512 devices in a mesh: pair: 16 (over y, core), ri: 8 (over z), batch: 4 (over x).
Axes of the slice: x: 4, y: 8, z: 8, core: 2. Of those that a mesh axis runs over, the one named last changes fastest.
Arguments:
- three_centre: float32 [512, 16, 128, 128], P('pair', 'ri'), may hold values from -0.13258252 to 0.13258252
- pair_mu: int32 [512], P('pair'), may hold values from 0 to 15
- pair_nu: int32 [512], P('pair'), may hold values from 0 to 15
- live_counts: int32 [16], P('pair'), may hold values from 1 to 32, 320 in all
- orbitals: float32 [2048, 512], P('pair', 'batch'), may hold values from -0.5 to 0.5
- metric: float32 [16, 16], P('ri'), may hold values from -1.5 to 1.5
Outputs:
- exchange_blocks: float32 [512, 128, 128], P('pair', ('ri', 'batch'))
The draws below stay inside these ranges and needn't reach their ends.
Inputs may be any that keep to these rules, and one draw needn't show every extreme that they name: `live_counts`: live slots of each list; the busiest list is full.
All inputs are finite; a program needn't handle non-finite values. No bound on the sum of `live_counts` on one device may be relied on, other than what follows from the above.
Results may differ from the reference program's by a relative error of at most 0.0001.
Values sent between devices are 32-bit elements; how exact they have to be, the bound alone decides.
A program may use at most 64 MiB of HBM per device.

```python
import math
import jax
import jax.numpy as jnp
import numpy as np
from jax import lax

BS = 128
LIST_DEV = 32
NBLK = 16
NAO = 2048
NRI = 16
NOCC = 512
PAIRS = 512
N_PAIR = 16


def set_ends(result, rng, least, largest):
    extent = result.shape
    index_at = [jax.random.randint(jax.random.fold_in(rng, axis), (), 0, extent[axis]) for axis in range(len(extent))]
    result = result.at[tuple(index_at)].set(least)
    longest = extent.index(max(extent))
    index_at[longest] = (index_at[longest] + 1) % extent[longest]
    return result.at[tuple(index_at)].set(largest)


def steps_of(stream_key, extent, split, low, high):
    loudness, own = 1.0, jax.random.fold_in(stream_key, 6)
    for position, shards_of in split:
        steps = jnp.exp(jax.random.uniform(jax.random.fold_in(own, position), (shards_of,), jnp.float32, low / len(split), high / len(split)))
        loudness = loudness * jnp.repeat(steps, extent[position] // shards_of).reshape([-1 if axis == position else 1 for axis in range(len(extent))])
    return loudness


def split_up(number_of, total, bound, slope):
    weights = [(1 << 20) // math.isqrt(standing ** slope) + 1 for standing in range(2, number_of + 1)]
    spare, given = total - bound - (number_of - 1), [1] * (number_of - 1)
    while spare > 0:
        movable = [i for i in range(number_of - 1) if given[i] < bound]
        pool, left = sum([weights[i] for i in movable]), spare
        for i in movable:
            extra = min(bound - given[i], max(1, left * weights[i] // pool), spare)
            given[i] = given[i] + extra
            spare = spare - extra
    return np.array([bound] + given)


def ragged_sizes(own_key, count, total, limit, skew):
    if count == 2:
        one = jax.random.randint(own_key, (), max(1, total - limit), min(limit, total - 1) + 1)
        return jnp.stack([one, total - one])
    tallies = jnp.asarray(split_up(count, total, limit, skew), jnp.int32)
    couples = (count - 1) // 2
    source_of, sink = tallies[1:1 + 2 * couples:2], tallies[2:2 + 2 * couples:2]
    room = jnp.minimum(source_of - 1, limit - sink)
    moved = jax.random.randint(jax.random.fold_in(own_key, 1), (couples,), 0, 1 << 20) % (room + 1)
    tallies = tallies.at[1:1 + 2 * couples:2].set(source_of - moved).at[2:2 + 2 * couples:2].set(sink + moved)
    return tallies[jax.random.permutation(jax.random.fold_in(own_key, 2), count)]


def centred(rng, dims, spread, bound, split=(), held_as=jnp.bfloat16):
    values = spread * jax.random.normal(rng, dims, jnp.float32)
    if split:
        values = values * steps_of(rng, dims, split, -0.22, 0.18)
    return jnp.clip(values, -bound, bound).astype(held_as)


def setup_inputs(seed: int = 0) -> dict:
    splits = jax.random.split(jax.random.key(seed), 7)
    return {
        "three_centre": centred(splits[0], (PAIRS, NRI, BS, BS), (0.5 * (NRI * NOCC * LIST_DEV) ** -0.25), 0.13258252, ((0, 16), (1, 8)), jnp.float32),
        "pair_mu": set_ends(jax.random.randint(splits[1], (PAIRS,), 0, NBLK), jax.random.fold_in(splits[1], 1), 0, NBLK - 1).astype(jnp.int32),
        "pair_nu": set_ends(jax.random.randint(splits[2], (PAIRS,), 0, NBLK), jax.random.fold_in(splits[2], 1), 0, NBLK - 1).astype(jnp.int32),
        "live_counts": ragged_sizes(splits[3], N_PAIR, LIST_DEV * N_PAIR * 5 // 8, LIST_DEV, 2).astype(jnp.int32),
        "orbitals": centred(splits[4], (NAO, NOCC), BS ** -0.5, 0.5, ((0, 16), (1, 4)), jnp.float32),
        "metric": centred(splits[5], (NRI, NRI), NRI ** -0.5, 1.5, ((0, 8),), jnp.float32),
    }


highest = lax.Precision.HIGHEST


def reference(three_centre, pair_mu, pair_nu, live_counts, orbitals, metric):
    pair_total = three_centre.shape[0]
    list_length = pair_total // live_counts.shape[0]
    block_count = orbitals.shape[0] // BS
    occupied = orbitals.shape[1]
    orbital_blocks = orbitals.reshape(block_count, BS, occupied)
    slot_index = jnp.arange(pair_total, dtype=jnp.int32)
    alive_mask = ((slot_index % list_length) < jnp.repeat(live_counts, list_length)).astype(jnp.float32)

    def add_entry(half_sums, entry_data):
        tensor_part, mu_index, nu_index, kept_mask = entry_data
        nu_rows = lax.dynamic_index_in_dim(orbital_blocks, nu_index, 0, keepdims=False)
        product = jnp.einsum("pmn,ni->pmi", tensor_part, nu_rows, precision=highest) * kept_mask
        return half_sums.at[mu_index].add(product), None

    start_sums = jnp.zeros((block_count, NRI, BS, occupied), jnp.float32)
    half_sums, _ = lax.scan(add_entry, start_sums, (three_centre, pair_mu, pair_nu, alive_mask))
    fitted = jnp.einsum("qp,apmi->aqmi", metric, half_sums, precision=highest)

    def one_block(entry_data):
        mu_index, nu_index, kept_mask = entry_data
        left_side = lax.dynamic_index_in_dim(fitted, mu_index, 0, keepdims=False)
        right_side = lax.dynamic_index_in_dim(fitted, nu_index, 0, keepdims=False)
        return jnp.einsum("qmi,qni->mn", left_side, right_side, precision=highest) * kept_mask

    return lax.map(one_block, (pair_mu, pair_nu, alive_mask))
```

```python
import functools

import jax
import jax.numpy as jnp
from jax import lax
from jax.experimental import pallas as pl
from jax.experimental.pallas import tpu as pltpu
from jax.sharding import PartitionSpec as P

MESH = pl.DeviceIdType.MESH
F32 = jnp.float32
BF16 = jnp.bfloat16
SLOTS = 32
NB = 16
BS = 128
NY, NZ, NX = 8, 8, 4
GROUP = 4
NEAR_FIRST = (1, 7, 2, 6, 3, 5, 4)
FAR_FIRST = (4, 3, 5, 2, 6, 1, 7, 0)


def split(x):
    hi = x.astype(BF16)
    return hi, (x - hi.astype(F32)).astype(BF16)


def mm(a, b, nt):
    dims = (((1,), (1 if nt else 0,)), ((), ()))
    return lax.dot_general(a, b, dims, preferred_element_type=F32)


def dot3(a, b, nt=False):
    (ah, al), (bh, bl) = a, b
    return mm(ah, bh, nt) + (mm(ah, bl, nt) + mm(al, bh, nt))


def kernel(
    mu_s, nu_s, prev_s, last_s, live_s, t_any, c_ref, kr_ref, o_ref,
    t_v, t_hi, t_lo, run, c_raw, c_hi, c_lo, kr_all, d_send, d_recv, ring, ho, hz, lb, rb, pk, xr, kf,
    t_sem, a_s, a_r, ad_s, ad_r, m_s, m_r, d_s, d_r, g_s, g_r, z_s, z_r,
    fy_s, fy_r, fz_s, fz_r, fd_s, fd_r, x_s, x_r, k_s, k_r, kd_s, kd_r,
):
    p, q, b = lax.axis_index("pair"), lax.axis_index("ri"), lax.axis_index("batch")
    y, c = p // 2, lax.rem(p, 2)

    def ypos(d):
        return lax.rem(y + d + NY, NY)

    def ydev(d):
        return (ypos(d) * 2 + c, q, b)

    def zpos(d):
        return lax.rem(q + d + NZ, NZ)

    def zdev(d):
        return (p, zpos(d), b)

    def xdev(d):
        return (p, q, lax.rem(b + d + NX, NX))

    partner = (y * 2 + 1 - c, q, b)
    sent = []

    def send(src, dst, ss, rs, dev):
        cp = pltpu.make_async_remote_copy(
            src_ref=src, dst_ref=dst, send_sem=ss, recv_sem=rs, device_id=dev, device_id_type=MESH
        )
        cp.start()
        sent.append(cp)
        return cp

    t_copy = pltpu.make_async_copy(t_any, t_v, t_sem)
    t_copy.start()
    barrier = pltpu.get_barrier_semaphore()
    peers = [ydev(d) for d in range(1, NY)] + [zdev(d) for d in range(1, NZ)]
    peers += [xdev(d) for d in range(1, NX)] + [partner]
    for dev in peers:
        pl.semaphore_signal(barrier, inc=1, device_id=dev, device_id_type=MESH)
    pl.semaphore_wait(barrier, len(peers))

    a_cp = {d: send(c_ref, c_raw.at[p], a_s.at[d], a_r.at[d], ydev(d)) for d in NEAR_FIRST}
    ad_cp = {0: send(c_ref, c_raw.at[p], ad_s.at[0], ad_r.at[0], partner)}
    m_cp = {d: send(kr_ref, kr_all.at[q], m_s.at[d], m_r.at[d], zdev(d)) for d in NEAR_FIRST}
    kr_all[q] = kr_ref[...]
    c_hi[p], c_lo[p] = split(c_ref[...])
    t_copy.wait()

    def split_t(k, carry):
        t_hi[k], t_lo[k] = split(t_v[k].reshape(2 * BS, BS))
        return carry

    lax.fori_loop(0, SLOTS, split_t, 0)
    run[SLOTS] = jnp.zeros((2 * BS, BS), F32)

    def take_c(i):
        c_hi[i], c_lo[i] = split(c_raw[i])

    for d in NEAR_FIRST:
        i = ypos(-d) * 2 + c
        a_cp[d].wait_recv()
        ad_cp[d] = send(c_raw.at[i], c_raw.at[i], ad_s.at[d], ad_r.at[d], partner)
        take_c(i)
    for d in (0,) + NEAR_FIRST:
        ad_cp[d].wait_recv()
        take_c(ypos(-d) * 2 + 1 - c)

    def add_slots(g, carry):
        products = []
        for j in range(GROUP):
            k = g * GROUP + j
            nu = nu_s[k]
            products.append(dot3((t_hi[k], t_lo[k]), (c_hi[nu], c_lo[nu])))
        for j in range(GROUP):
            k = g * GROUP + j
            run[k] = products[j] + run[prev_s[k]]
        return carry

    lax.fori_loop(0, SLOTS // GROUP, add_slots, 0)

    d_cp = {}
    for off in FAR_FIRST:
        d_send[off] = run[last_s[ypos(off) * 2 + 1 - c]].reshape(2, BS, BS)
        d_cp[off] = send(d_send.at[off], d_recv.at[off], d_s.at[off], d_r.at[off], partner)

    def add_core(off):
        d_cp[off].wait_recv()
        d_recv[off] = d_recv[off] + run[last_s[ypos(off) * 2 + c]].reshape(2, BS, BS)

    half = BS // 2
    g_cp = {}
    add_core(4)
    for s in range(1, 5):
        for way in (0, 1):
            off = 5 - s if way == 0 else 3 + s
            if s > 1:
                add_core(off)
            for part in (0, 1):
                if s > 1:
                    g_cp[part, way, s - 1].wait_recv()
                rows = pl.ds(half * way, half) if s <= 2 else pl.ds(0, BS)
                if s > 1:
                    d_recv[off, part, rows, :] = d_recv[off, part, rows, :] + ring[part, way, s - 2, rows, :]
                if s > 1:
                    rows = pl.ds(0, BS)
                n = (part * 2 + way) * 4 + s - 1
                g_cp[part, way, s] = send(
                    d_recv.at[off, part, rows], ring.at[part, way, s - 1, rows],
                    g_s.at[n], g_r.at[n], ydev(1 if way == 0 else -1),
                )
    add_core(0)
    for part in (0, 1):
        for way in (0, 1):
            g_cp[part, way, 4].wait_recv()
        ho[part] = d_recv[0, part] + (ring[part, 0, 3] + ring[part, 1, 3])

    z_cp = {}
    for d in NEAR_FIRST:
        rows = pl.ds(pl.multiple_of(zpos(d) * 16, 16), 16)
        z_cp[d] = send(ho.at[:, rows], hz.at[q], z_s.at[d], z_r.at[d], zdev(d))
    hz[q] = ho[:, pl.ds(pl.multiple_of(q * 16, 16), 16), :]
    for d in NEAR_FIRST:
        m_cp[d].wait_recv()
    mixer = split(kr_all[...].reshape(256, 256))
    for d in NEAR_FIRST:
        z_cp[d].wait_recv()
    fitted = dot3(mixer, split(hz[...].reshape(256, BS)))
    lb[p] = fitted
    rb[q] = fitted

    f_cp = {}
    fd_cp = {}

    def hops(way, part):
        return 4 if way == part else 3

    def fitted_slot(axis, way, s):
        d = 1 - s if way == 0 else s - 1
        return ypos(d) * 2 + c if axis == 0 else zpos(d)

    def to_partner(way, part, s):
        rows = pl.ds(part * BS, BS)
        i = fitted_slot(0, way, s)
        n = (4 + (1 - s if way == 0 else s - 1)) % 8 * 2 + part
        fd_cp[n] = send(lb.at[i, rows], lb.at[i, rows], fd_s.at[n], fd_r.at[n], partner)

    for s in range(1, 6):
        for part in (0, 1):
            for way in (part, 1 - part):
                if s > hops(way, part) + 1:
                    continue
                for axis in (0, 1):
                    if s > 1:
                        f_cp[axis, way, part, s - 1].wait_recv()
                    if s <= hops(way, part):
                        rows = pl.ds(part * BS, BS)
                        i = fitted_slot(axis, way, s)
                        buf, ss, rs = ((lb, fy_s, fy_r), (rb, fz_s, fz_r))[axis]
                        n = (part * 2 + way) * 4 + s - 1
                        step = 1 if way == 0 else -1
                        f_cp[axis, way, part, s] = send(
                            buf.at[i, rows], buf.at[i, rows], ss.at[n], rs.at[n],
                            ydev(step) if axis == 0 else zdev(step),
                        )
                if s > 1 or way == 0:
                    to_partner(way, part, s)
    for n in sorted(fd_cp):
        fd_cp[n].wait_recv()

    def add_q(i, acc):
        rows = pl.ds(pl.multiple_of(i * 16, 16), 16)
        left = lb[:, rows, :].reshape(256, BS)
        right = rb[:, rows, :].reshape(BS, BS)
        return acc + dot3(split(left), split(right), nt=True)

    k_part = lax.fori_loop(0, 16, add_q, jnp.zeros((256, BS), F32))
    tiles = k_part.reshape(16, 2, 8, BS)
    low = lax.broadcasted_iota(jnp.int32, (8, BS), 0) < 4
    for j in range(NX):
        for pair in range(8):
            first, second = tiles[2 * pair, j // 2], tiles[2 * pair + 1, j // 2]
            if j % 2 == 0:
                tile = jnp.where(low, first, pltpu.roll(second, 4, 0))
            else:
                tile = jnp.where(low, pltpu.roll(first, 4, 0), second)
            pk[j, pair] = tile
    x_cp = {}
    for d in range(1, NX):
        to = lax.rem(b + d, NX)
        x_cp[d] = send(pk.at[to], xr.at[d], x_s.at[d], x_r.at[d], xdev(d))
    for d in range(1, NX):
        x_cp[d].wait_recv()
    kf[p] = (pk[b] + xr[1]) + (xr[2] + xr[3])

    k_cp = {d: send(kf.at[p], kf.at[p], k_s.at[d], k_r.at[d], ydev(d)) for d in NEAR_FIRST}
    kd_cp = {0: send(kf.at[p], kf.at[p], kd_s.at[0], kd_r.at[0], partner)}
    for d in NEAR_FIRST:
        i = ypos(-d) * 2 + c
        k_cp[d].wait_recv()
        kd_cp[d] = send(kf.at[i], kf.at[i], kd_s.at[d], kd_r.at[d], partner)
    for d in (0,) + NEAR_FIRST:
        kd_cp[d].wait_recv()

    live = live_s[0]
    for k in range(SLOTS):
        mu = mu_s[k]
        tile = kf[nu_s[k], mu >> 1]
        rows = jnp.where(mu & 1 == 1, tile[4:8], tile[0:4])
        o_ref[k] = jnp.where(k < live, rows, jnp.zeros_like(rows))

    for cp in sent:
        cp.wait_send()


def per_device(three_centre, pair_mu, pair_nu, live_counts, orbitals, metric):
    slot = jnp.arange(SLOTS, dtype=jnp.int32)
    alive = slot < live_counts[0]
    same = (pair_mu[:, None] == pair_mu[None, :]) & alive[None, :] & (slot[None, :] < slot[:, None])
    prev = jnp.max(jnp.where(same, slot[None, :], -1), axis=1)
    prev = jnp.where(prev < 0, SLOTS, prev)
    block = jnp.arange(NB, dtype=jnp.int32)
    mine = (pair_mu[None, :] == block[:, None]) & alive[None, :]
    last = jnp.max(jnp.where(mine, slot[None, :], -1), axis=1)
    last = jnp.where(last < 0, SLOTS, last)
    wide = jnp.broadcast_to(metric[:, :, None], (2, 16, 16)).reshape(2, 1, 256)
    row = jnp.arange(16, dtype=jnp.int32)[None, :, None]
    col = jnp.arange(256, dtype=jnp.int32)[None, None, :] % 16
    mixer = jnp.where(row == col, wide, 0.0).reshape(32, 256)
    smem = pl.BlockSpec(memory_space=pltpu.SMEM)
    vmem = pl.BlockSpec(memory_space=pltpu.VMEM)

    def sems(*counts):
        return [pltpu.SemaphoreType.DMA((n,)) for n in counts for _ in range(2)]

    return pl.pallas_call(
        kernel,
        out_shape=jax.ShapeDtypeStruct((SLOTS, 4, BS), F32),
        in_specs=[smem] * 5 + [pl.BlockSpec(memory_space=pl.ANY), vmem, vmem],
        out_specs=vmem,
        scratch_shapes=[
            pltpu.VMEM((SLOTS, 2, BS, BS), F32),
            pltpu.VMEM((SLOTS, 2 * BS, BS), BF16),
            pltpu.VMEM((SLOTS, 2 * BS, BS), BF16),
            pltpu.VMEM((SLOTS + 1, 2 * BS, BS), F32),
            pltpu.VMEM((NB, BS, BS), F32),
            pltpu.VMEM((NB, BS, BS), BF16),
            pltpu.VMEM((NB, BS, BS), BF16),
            pltpu.VMEM((NZ, 32, 256), F32),
            pltpu.VMEM((NY, 2, BS, BS), F32),
            pltpu.VMEM((NY, 2, BS, BS), F32),
            pltpu.VMEM((2, 2, 4, BS, BS), F32),
            pltpu.VMEM((2, BS, BS), F32),
            pltpu.VMEM((NZ, 2, 16, BS), F32),
            pltpu.VMEM((NB, 256, BS), F32),
            pltpu.VMEM((NZ, 256, BS), F32),
            pltpu.VMEM((NX, 8, 8, BS), F32),
            pltpu.VMEM((NX, 8, 8, BS), F32),
            pltpu.VMEM((NB, 8, 8, BS), F32),
            pltpu.SemaphoreType.DMA,
        ]
        + sems(8, 8, 8, 8, 16, 8, 16, 16, 16, 4, 8, 8),
        compiler_params=pltpu.CompilerParams(
            collective_id=0, has_side_effects=True, vmem_limit_bytes=48 * 2**20
        ),
        name="exchange",
    )(pair_mu, pair_nu, prev, last, live_counts, three_centre, orbitals, mixer)


def solution(mesh):
    in_specs = (
        P("pair", "ri", None, None),
        P("pair"),
        P("pair"),
        P("pair"),
        P("pair", "batch"),
        P("ri", None),
    )
    return jax.shard_map(
        per_device,
        mesh=mesh,
        in_specs=in_specs,
        out_specs=P("pair", ("ri", "batch"), None),
        check_vma=False,
    )
```

```python
import jax
import jax.numpy as jnp
from jax import lax
from jax.experimental import pallas as pl
from jax.experimental.pallas import tpu as pltpu
from jax.sharding import PartitionSpec as P

MESH = pl.DeviceIdType.MESH
F32 = jnp.float32
BF16 = jnp.bfloat16
SLOTS = 32
NB = 16
BS = 128
NY, NZ, NX = 8, 8, 4
GROUP = 4
NEAR_FIRST = (1, 7, 2, 6, 3, 5, 4)


def split(x):
    hi = x.astype(BF16)
    return hi, (x - hi.astype(F32)).astype(BF16)


def mm(a, b, nt=False):
    dims = (((1,), (1 if nt else 0,)), ((), ()))
    return lax.dot_general(a, b, dims, preferred_element_type=F32)


def kernel(
    mu_any, nu_any, live_any, t_any, c_any, m_any, o_ref,
    mu_s, nu_s, live_s, prev_s, last_s,
    t_v, t_cat, run, c_raw, c_cat, m_v, kr_own, kr_all, mix, d_send, d_recv, ring, ho, hz, lb, rb, l_cat, r_cat,
    pk, xr, kf,
    in_sem, a_s, a_r, ad_s, ad_r, m_s, m_r, d_s, d_r, g_s, g_r, z_s, z_r,
    fy_s, fy_r, fz_s, fz_r, fd_s, fd_r, x_s, x_r, k_s, k_r, kd_s, kd_r,
):
    p, q, b = lax.axis_index("pair"), lax.axis_index("ri"), lax.axis_index("batch")
    y, c = p // 2, lax.rem(p, 2)

    def ypos(d):
        return lax.rem(y + d + NY, NY)

    def ydev(d):
        return (ypos(d) * 2 + c, q, b)

    def zpos(d):
        return lax.rem(q + d + NZ, NZ)

    def zdev(d):
        return (p, zpos(d), b)

    def xdev(d):
        return (p, q, lax.rem(b + d + NX, NX))

    partner = (y * 2 + 1 - c, q, b)
    sent = []

    def send(src, dst, ss, rs, dev):
        cp = pltpu.make_async_remote_copy(
            src_ref=src, dst_ref=dst, send_sem=ss, recv_sem=rs, device_id=dev, device_id_type=MESH
        )
        cp.start()
        sent.append(cp)
        return cp

    def drain(keep=0):
        while len(sent) > keep:
            sent.pop(0).wait_send()

    def block(d):
        return ypos(d) * 2 + c

    def other(d):
        return ypos(d) * 2 + 1 - c

    class Gather:
        def __init__(self, own, buf, half, sems):
            self.buf, self.half, self.sems = buf, half, sems
            ss, rs, ds, dr = sems
            self.cp = {d: send(own, buf.at[p], ss.at[i], rs.at[i], ydev(d)) for i, d in enumerate((2, -2, 1, -1))}
            self.dp = {0: send(own, buf.at[p], ds.at[0], dr.at[0], partner)}

        def relay(self, d):
            step = d // 2
            ss, rs, _, _ = self.sems
            self.cp[d].wait_recv()
            n = 4 if step == 1 else 5
            at = self.buf.at[block(-d)]
            self.cp[3 * step] = send(at, at, ss.at[n], rs.at[n], ydev(step))
            rows = pl.ds(0 if step == 1 else self.half, self.half)
            part = self.buf.at[block(-d), rows]
            self.cp[4 * step] = send(part, part, ss.at[n + 2], rs.at[n + 2], ydev(d))
            self.share(d)

        def share(self, d):
            _, _, ds, dr = self.sems
            at = self.buf.at[block(-d)]
            self.dp[d] = send(at, at, ds.at[d % 8], dr.at[d % 8], partner)

        def take(self, d):
            self.cp[d].wait_recv()
            if d == 4:
                self.cp[-4].wait_recv()
            self.share(d)

        def shared(self, d):
            self.dp[d].wait_recv()

    ins = [
        pltpu.make_async_copy(src, dst, in_sem.at[i])
        for i, (src, dst) in enumerate(
            ((c_any, c_raw.at[p]), (mu_any, mu_s), (nu_any, nu_s), (live_any, live_s), (m_any, m_v), (t_any, t_v))
        )
    ]
    for cp in ins:
        cp.start()
    barrier = pltpu.get_barrier_semaphore()
    peers = [ydev(d) for d in (1, -1, 2, -2)] + [zdev(d) for d in range(1, NZ)]
    peers += [xdev(d) for d in range(1, NX)] + [partner]
    for dev in peers:
        pl.semaphore_signal(barrier, inc=1, device_id=dev, device_id_type=MESH)
    pl.semaphore_wait(barrier, len(peers))

    orbs = Gather(c_any, c_raw, BS // 2, (a_s, a_r, ad_s, ad_r))
    ins[4].wait()
    col = lax.broadcasted_iota(jnp.int32, (16, 256), 1)
    spot = (col % 16) == lax.broadcasted_iota(jnp.int32, (16, 256), 0)
    for j in range(2):
        wide = jnp.zeros((16, 256), F32)
        for i in range(16):
            wide = jnp.where((col >= 16 * i) & spot, m_v[pl.ds(j, 1), pl.ds(i, 1)], wide)
        kr_own[pl.ds(16 * j, 16), :] = wide
    kr_all[q] = kr_own[...]
    m_cp = {d: send(kr_own, kr_all.at[q], m_s.at[d], m_r.at[d], zdev(d)) for d in NEAR_FIRST}

    for i in (1, 2, 3):
        ins[i].wait()
    live = live_s[0]

    def link_slot(k, carry):
        mine = mu_s[k]
        best = jnp.int32(SLOTS)
        for j in range(SLOTS):
            best = jnp.where((mu_s[j] == mine) & (j < k), jnp.int32(j), best)
        prev_s[k] = best
        return carry

    def link_block(a, carry):
        best = jnp.int32(SLOTS)
        for j in range(SLOTS):
            best = jnp.where((mu_s[j] == a) & (j < live), jnp.int32(j), best)
        last_s[a] = best
        return carry

    lax.fori_loop(0, SLOTS, link_slot, 0)
    lax.fori_loop(0, NB, link_block, 0)

    def take_c(i):
        hi, lo = split(c_raw[i])
        for j in range(2):
            c_cat[i, pl.ds(BS * j, BS), pl.ds(0, BS)] = hi
            c_cat[i, pl.ds(BS * j, BS), pl.ds(BS, BS)] = lo

    def split_t(k, carry):
        hi, lo = split(t_v[k].reshape(2 * BS, BS))
        t_cat[k, :, pl.ds(0, BS)] = hi
        t_cat[k, :, pl.ds(BS, BS)] = lo
        return carry

    ins[5].wait()
    lax.fori_loop(0, 8, split_t, 0)
    for d in (2, -2):
        orbs.relay(d)
    for d in (1, -1):
        orbs.take(d)
    lax.fori_loop(8, SLOTS, split_t, 0)
    ins[0].wait()
    take_c(p)
    for d in (2, -2, 1, -1):
        take_c(block(-d))
    for d in (0, 2, -2, 1, -1):
        orbs.shared(d)
        take_c(other(-d))
    for d in (3, -3, 4):
        orbs.take(d)
        take_c(block(-d))
    run[SLOTS] = jnp.zeros((2 * BS, BS), F32)
    for d in (3, -3, 4):
        orbs.shared(d)
        take_c(other(-d))

    def add_slots(g, carry):
        products = []
        for j in range(GROUP):
            k = g * GROUP + j
            both = mm(t_cat[k], c_cat[nu_s[k]])
            products.append(both[:, :BS] + both[:, BS:])
        for j in range(GROUP):
            k = g * GROUP + j
            run[k] = products[j] + run[prev_s[k]]
        return carry

    lax.fori_loop(0, SLOTS // GROUP, add_slots, 0)

    d_cp = {}
    for off in (4, 3, 5, 2, 6, 1, 7, 0):
        d_send[off] = run[last_s[other(off)]].reshape(2, BS, BS)
        d_cp[off] = send(d_send.at[off], d_recv.at[off], d_s.at[off], d_r.at[off], partner)

    def add_core(off):
        d_cp[off].wait_recv()
        d_recv[off] = d_recv[off] + run[last_s[block(off)]].reshape(2, BS, BS)

    half = BS // 2
    g_cp = {}

    def pass_on(off, part, way, kind, hop):
        rows = pl.ds(half * way, half) if kind == 3 else pl.ds(0, BS)
        n = (part * 2 + way) * 4 + kind
        g_cp[part, way, kind] = send(
            d_recv.at[off, part, rows], ring.at[part, way, kind, rows], g_s.at[n], g_r.at[n],
            ydev(hop if way == 0 else -hop),
        )

    add_core(4)
    for part in (0, 1):
        for way in (0, 1):
            pass_on(4, part, way, 3, 2)
    for way, off in ((0, 3), (1, 5)):
        add_core(off)
        for part in (0, 1):
            pass_on(off, part, way, 0, 1)
    add_core(2)
    add_core(6)
    for part in (0, 1):
        for way, off in ((0, 2), (1, 6)):
            g_cp[part, way, 3].wait_recv()
            rows = pl.ds(half * way, half)
            d_recv[off, part, rows, :] = d_recv[off, part, rows, :] + ring[part, way, 3, rows, :]
            g_cp[part, way, 0].wait_recv()
            d_recv[off, part] = d_recv[off, part] + ring[part, way, 0]
            pass_on(off, part, way, 1, 1)
    add_core(1)
    add_core(7)
    add_core(0)
    for part in (0, 1):
        for way, off in ((0, 1), (1, 7)):
            g_cp[part, way, 1].wait_recv()
            d_recv[off, part] = d_recv[off, part] + ring[part, way, 1]
            pass_on(off, part, way, 2, 1)
    for d in NEAR_FIRST:
        m_cp[d].wait_recv()
    mix_hi, mix_lo = split(kr_all[...].reshape(256, 256))
    mix[0] = mix_hi
    mix[1] = mix_lo

    z_cp = {}
    for part in (0, 1):
        for way in (0, 1):
            g_cp[part, way, 2].wait_recv()
        ho[part] = d_recv[0, part] + (ring[part, 0, 2] + ring[part, 1, 2])
        for d in NEAR_FIRST:
            rows = pl.ds(pl.multiple_of(zpos(d) * 16, 16), 16)
            n = d * 2 + part
            z_cp[n] = send(ho.at[part, rows], hz.at[q, part], z_s.at[n], z_r.at[n], zdev(d))
        hz[q, part] = ho[part, pl.ds(pl.multiple_of(q * 16, 16), 16), :]
    drain(14)
    for n in sorted(z_cp):
        z_cp[n].wait_recv()
    hz_hi, hz_lo = split(hz[...].reshape(256, BS))
    fitted = mm(mix[0], hz_hi) + (mm(mix[0], hz_lo) + mm(mix[1], hz_hi))
    lb[p] = fitted
    rb[q] = fitted

    f_cp = {}
    fd_cp = {}

    def hand_on(axis, way, part, d, kind, hop):
        sign = 1 if way == 0 else -1
        buf, ss, rs = ((lb, fy_s, fy_r), (rb, fz_s, fz_r))[axis]
        i = block(-sign * d) if axis == 0 else zpos(-sign * d)
        at = buf.at[i, pl.ds(part * BS, BS)]
        n = (part * 2 + way) * 4 + kind
        dev = ydev(sign * hop) if axis == 0 else zdev(sign * hop)
        f_cp[axis, way, part, kind] = send(at, at, ss.at[n], rs.at[n], dev)

    def to_partner(d, part):
        at = lb.at[block(-d), pl.ds(part * BS, BS)]
        n = (d % 8) * 2 + part
        fd_cp[d % 8, part] = send(at, at, fd_s.at[n], fd_r.at[n], partner)

    def put_left(i, part):
        hi, lo = split(lb[i, pl.ds(part * BS, BS), :])
        rows = pl.ds(pl.multiple_of(i * 16, 16), 16)
        for j in range(8):
            at = (part * 8 + j) * 256
            l_cat[rows, pl.ds(at, BS)] = hi[16 * j : 16 * j + 16]
            l_cat[rows, pl.ds(at + BS, BS)] = lo[16 * j : 16 * j + 16]

    def put_right(i, part):
        hi, lo = split(rb[i, pl.ds(part * BS, BS), :])
        for s, x in enumerate((hi, lo)):
            rows = pl.ds(pl.multiple_of(i * 16 + BS * s, 16), 16)
            for j in range(8):
                at = (part * 8 + j) * 256
                r_cat[rows, pl.ds(at, BS)] = x[16 * j : 16 * j + 16]
                r_cat[rows, pl.ds(at + BS, BS)] = x[16 * j : 16 * j + 16]

    def put(axis, d, part):
        if axis == 0:
            put_left(block(-d), part)
        else:
            put_right(zpos(-d), part)

    def put_shared(d, part):
        fd_cp[d % 8, part].wait_recv()
        put_left(other(-d), part)

    for part in (0, 1):
        for way in (0, 1):
            for axis in (0, 1):
                hand_on(axis, way, part, 0, 0, 1)
    for part in (0, 1):
        to_partner(0, part)
    for part in (0, 1):
        put(0, 0, part)
        put(1, 0, part)
    for part in (0, 1):
        for way, sign in ((0, 1), (1, -1)):
            for axis in (0, 1):
                f_cp[axis, way, part, 0].wait_recv()
                hand_on(axis, way, part, 1, 1, 1)
                if axis == 0:
                    to_partner(sign, part)
    for part in (0, 1):
        for sign in (1, -1):
            for axis in (0, 1):
                put(axis, sign, part)
        put_shared(0, part)
    for part in (0, 1):
        for way, sign in ((0, 1), (1, -1)):
            for axis in (0, 1):
                f_cp[axis, way, part, 1].wait_recv()
                hand_on(axis, way, part, 2, 2, 1)
                if way == part:
                    hand_on(axis, way, part, 2, 3, 2)
                if axis == 0:
                    to_partner(2 * sign, part)
    for part in (0, 1):
        for sign in (1, -1):
            put_shared(sign, part)
            for axis in (0, 1):
                put(axis, 2 * sign, part)
    for part in (0, 1):
        for kind in (2, 3):
            for way, sign in ((0, 1), (1, -1)):
                if kind == 3 and way != part:
                    continue
                for axis in (0, 1):
                    f_cp[axis, way, part, kind].wait_recv()
                    if axis == 0:
                        to_partner((kind + 1) * sign, part)
                    put(axis, (kind + 1) * sign, part)
        for d in (2, -2):
            put_shared(d, part)

    k_part = None
    for part in (0, 1):
        for d in (3, -3, 4):
            put_shared(d, part)
        lanes = pl.ds(part * 2048, 2048)
        both = mm(l_cat[:, lanes], r_cat[:, lanes], nt=True)
        both = both[:, :BS] + both[:, BS:]
        k_part = both if part == 0 else k_part + both
    tiles = k_part.reshape(16, 2, 8, BS)
    low = lax.broadcasted_iota(jnp.int32, (8, BS), 0) < 4
    for j in range(NX):
        for pair in range(8):
            first, second = tiles[2 * pair, j // 2], tiles[2 * pair + 1, j // 2]
            if j % 2 == 0:
                tile = jnp.where(low, first, pltpu.roll(second, 4, 0))
            else:
                tile = jnp.where(low, pltpu.roll(first, 4, 0), second)
            pk[j, pair] = tile
    x_cp = {}
    for d in range(1, NX):
        to = lax.rem(b + d, NX)
        x_cp[d] = send(pk.at[to], xr.at[d], x_s.at[d], x_r.at[d], xdev(d))
    drain(3)
    for d in range(1, NX):
        x_cp[d].wait_recv()
    kf[p] = (pk[b] + xr[1]) + (xr[2] + xr[3])

    cols = Gather(kf.at[p], kf, 4, (k_s, k_r, kd_s, kd_r))
    for d in (2, -2):
        cols.relay(d)
    for d in (1, -1, 3, -3, 4):
        cols.take(d)
    for d in (0, 2, -2, 1, -1, 3, -3, 4):
        cols.shared(d)

    for k in range(SLOTS):
        mu = mu_s[k]
        tile = kf[nu_s[k], mu >> 1]
        rows = jnp.where(mu & 1 == 1, tile[4:8], tile[0:4])
        o_ref[k] = jnp.where(k < live, rows, jnp.zeros_like(rows))
    drain()


def per_device(three_centre, pair_mu, pair_nu, live_counts, orbitals, metric):
    hbm = pl.BlockSpec(memory_space=pltpu.HBM)

    def sems(*counts):
        return [pltpu.SemaphoreType.DMA((n,)) for n in counts for _ in range(2)]

    return pl.pallas_call(
        kernel,
        out_shape=jax.ShapeDtypeStruct((SLOTS, 4, BS), F32),
        in_specs=[hbm] * 6,
        out_specs=pl.BlockSpec(memory_space=pltpu.VMEM),
        scratch_shapes=[
            pltpu.SMEM((SLOTS,), jnp.int32),
            pltpu.SMEM((SLOTS,), jnp.int32),
            pltpu.SMEM((1,), jnp.int32),
            pltpu.SMEM((SLOTS,), jnp.int32),
            pltpu.SMEM((NB,), jnp.int32),
            pltpu.VMEM((SLOTS, 2, BS, BS), F32),
            pltpu.VMEM((SLOTS, 2 * BS, 2 * BS), BF16),
            pltpu.VMEM((SLOTS + 1, 2 * BS, BS), F32),
            pltpu.VMEM((NB, BS, BS), F32),
            pltpu.VMEM((NB, 2 * BS, 2 * BS), BF16),
            pltpu.VMEM((2, 16), F32),
            pltpu.VMEM((32, 256), F32),
            pltpu.VMEM((NZ, 32, 256), F32),
            pltpu.VMEM((2, 256, 256), BF16),
            pltpu.VMEM((NY, 2, BS, BS), F32),
            pltpu.VMEM((NY, 2, BS, BS), F32),
            pltpu.VMEM((2, 2, 4, BS, BS), F32),
            pltpu.VMEM((2, BS, BS), F32),
            pltpu.VMEM((NZ, 2, 16, BS), F32),
            pltpu.VMEM((NB, 256, BS), F32),
            pltpu.VMEM((NZ, 256, BS), F32),
            pltpu.VMEM((256, 4096), BF16),
            pltpu.VMEM((256, 4096), BF16),
            pltpu.VMEM((NX, 8, 8, BS), F32),
            pltpu.VMEM((NX, 8, 8, BS), F32),
            pltpu.VMEM((NB, 8, 8, BS), F32),
            pltpu.SemaphoreType.DMA((6,)),
        ]
        + sems(8, 8, 8, 8, 16, 16, 16, 16, 16, 4, 8, 8),
        compiler_params=pltpu.CompilerParams(
            collective_id=0, has_side_effects=True, vmem_limit_bytes=56 * 2**20
        ),
        name="exchange",
    )(pair_mu, pair_nu, live_counts, three_centre, orbitals, metric)


def solution(mesh):
    in_specs = (
        P("pair", "ri", None, None),
        P("pair"),
        P("pair"),
        P("pair"),
        P("pair", "batch"),
        P("ri", None),
    )
    return jax.shard_map(
        per_device,
        mesh=mesh,
        in_specs=in_specs,
        out_specs=P("pair", ("ri", "batch"), None),
        check_vma=False,
    )
```

```python
import jax
import jax.numpy as jnp
from jax import lax
from jax.experimental import pallas as pl
from jax.experimental.pallas import tpu as pltpu
from jax.sharding import PartitionSpec as P

MESH = pl.DeviceIdType.MESH
F32 = jnp.float32
BF16 = jnp.bfloat16
SLOTS = 32
NB = 16
BS = 128
NY, NZ, NX = 8, 8, 4
GROUP = 4
FAR_FIRST = (4, 3, 5, 2, 6, 1, 7)


def split(x):
    hi = x.astype(BF16)
    return hi, (x - hi.astype(F32)).astype(BF16)


def mm(a, b, nt=False):
    dims = (((1,), (1 if nt else 0,)), ((), ()))
    return lax.dot_general(a, b, dims, preferred_element_type=F32)


def kernel(
    mu_any, nu_any, live_any, t_any, c_any, m_any, o_ref,
    mu_s, nu_s, live_s, prev_s, last_s,
    t_v, t_cat, run, c_raw, c_cat, m_v, kr_own, kr_all, mix, d_send, d_recv, ring, ho, hz, lb, rb, l_cat, r_cat,
    pk, xr, kf,
    in_sem, a_s, a_r, ad_s, ad_r, m_s, m_r, d_s, d_r, g_s, g_r, z_s, z_r,
    fy_s, fy_r, fz_s, fz_r, fd_s, fd_r, x_s, x_r, k_s, k_r, kd_s, kd_r,
):
    p, q, b = lax.axis_index("pair"), lax.axis_index("ri"), lax.axis_index("batch")
    y, c = p // 2, lax.rem(p, 2)

    def ypos(d):
        return lax.rem(y + d + NY, NY)

    def ydev(d):
        return (ypos(d) * 2 + c, q, b)

    def zpos(d):
        return lax.rem(q + d + NZ, NZ)

    def zdev(d):
        return (p, zpos(d), b)

    def xdev(d):
        return (p, q, lax.rem(b + d + NX, NX))

    partner = (y * 2 + 1 - c, q, b)
    sent = []

    def send(src, dst, ss, rs, dev):
        cp = pltpu.make_async_remote_copy(
            src_ref=src, dst_ref=dst, send_sem=ss, recv_sem=rs, device_id=dev, device_id_type=MESH
        )
        cp.start()
        sent.append(cp)
        return cp

    def drain(keep=0):
        while len(sent) > keep:
            sent.pop(0).wait_send()

    def block(d):
        return ypos(d) * 2 + c

    def other(d):
        return ypos(d) * 2 + 1 - c

    class Gather:
        def __init__(self, piece, whole, buf, half, sems):
            self.piece, self.whole, self.buf, self.half, self.sems = piece, whole, buf, half, sems
            self.cp, self.dp = {}, {}

        def post(self, key, src, dst, d):
            ss, rs, _, _ = self.sems
            n = len(self.cp)
            self.cp[key] = send(src, dst, ss.at[n], rs.at[n], ydev(d))

        def at(self, i, h):
            return self.buf.at[i, pl.ds(self.half * h, self.half)]

        def far(self, turn):
            for s in (1, -1):
                h = turn if s == 1 else 1 - turn
                self.post((2 * s, h), self.piece(h), self.at(p, h), 2 * s)

        def near(self):
            for s in (1, -1):
                self.post(s, self.whole, self.buf.at[p], s)
            self.share(0, self.whole)

        def relay(self, turn):
            for s in (1, -1):
                h = turn if s == 1 else 1 - turn
                self.cp[2 * s, h].wait_recv()
                at = self.at(block(-2 * s), h)
                if turn == 0:
                    self.post(4 * s, at, at, 2 * s)
                self.post((3 * s, h), at, at, s)
            if turn == 1:
                self.share(2)
                self.share(-2)

        def share(self, d, src=None):
            _, _, ds, dr = self.sems
            at = self.buf.at[block(-d)]
            self.dp[d] = send(at if src is None else src, at, ds.at[d % 8], dr.at[d % 8], partner)

        def take(self, d):
            for key in {1: (1,), -1: (-1,), 3: ((3, 0), (3, 1)), -3: ((-3, 1), (-3, 0)), 4: (4, -4)}[d]:
                self.cp[key].wait_recv()
            self.share(d)

        def shared(self, d):
            self.dp[d].wait_recv()

    ins = [
        pltpu.make_async_copy(src, dst, in_sem.at[i])
        for i, (src, dst) in enumerate(
            ((c_any, c_raw.at[p]), (mu_any, mu_s), (nu_any, nu_s), (live_any, live_s), (m_any, m_v), (t_any, t_v))
        )
    ]
    for cp in ins:
        cp.start()
    barrier = pltpu.get_barrier_semaphore()
    peers = [ydev(d) for d in (1, -1, 2, -2)] + [zdev(d) for d in range(1, NZ)]
    peers += [xdev(d) for d in range(1, NX)] + [partner]
    for dev in peers:
        pl.semaphore_signal(barrier, inc=1, device_id=dev, device_id_type=MESH)
    pl.semaphore_wait(barrier, len(peers))

    half = BS // 2
    orbs = Gather(lambda h: c_any.at[pl.ds(half * h, half)], c_any, c_raw, half, (a_s, a_r, ad_s, ad_r))
    orbs.far(0)
    orbs.far(1)
    ins[4].wait()
    col = lax.broadcasted_iota(jnp.int32, (16, 256), 1)
    spot = (col % 16) == lax.broadcasted_iota(jnp.int32, (16, 256), 0)
    for j in range(2):
        wide = jnp.zeros((16, 256), F32)
        for i in range(16):
            wide = jnp.where((col >= 16 * i) & spot, m_v[pl.ds(j, 1), pl.ds(i, 1)], wide)
        kr_own[pl.ds(16 * j, 16), :] = wide
    kr_all[q] = kr_own[...]
    m_cp = {d: send(kr_own, kr_all.at[q], m_s.at[d], m_r.at[d], zdev(d)) for d in FAR_FIRST}
    orbs.near()

    for i in (1, 2, 3):
        ins[i].wait()
    live = live_s[0]

    def link_slot(k, carry):
        mine = mu_s[k]
        best = jnp.int32(SLOTS)
        for j in range(SLOTS):
            best = jnp.where((mu_s[j] == mine) & (j < k), jnp.int32(j), best)
        prev_s[k] = best
        return carry

    def link_block(a, carry):
        best = jnp.int32(SLOTS)
        for j in range(SLOTS):
            best = jnp.where((mu_s[j] == a) & (j < live), jnp.int32(j), best)
        last_s[a] = best
        return carry

    lax.fori_loop(0, SLOTS, link_slot, 0)
    lax.fori_loop(0, NB, link_block, 0)

    def take_c(i):
        hi, lo = split(c_raw[i])
        for j in range(2):
            c_cat[i, pl.ds(BS * j, BS), pl.ds(0, BS)] = hi
            c_cat[i, pl.ds(BS * j, BS), pl.ds(BS, BS)] = lo

    def split_t(k, carry):
        hi, lo = split(t_v[k].reshape(2 * BS, BS))
        t_cat[k, :, pl.ds(0, BS)] = hi
        t_cat[k, :, pl.ds(BS, BS)] = lo
        return carry

    ins[5].wait()
    lax.fori_loop(0, 8, split_t, 0)
    orbs.relay(0)
    orbs.relay(1)
    for d in (1, -1):
        orbs.take(d)
    lax.fori_loop(8, SLOTS, split_t, 0)
    ins[0].wait()
    take_c(p)
    for d in (2, -2, 1, -1):
        take_c(block(-d))
    for d in (0, 2, -2, 1, -1):
        orbs.shared(d)
        take_c(other(-d))
    for d in (3, -3, 4):
        orbs.take(d)
        take_c(block(-d))
    run[SLOTS] = jnp.zeros((2 * BS, BS), F32)
    for d in (3, -3, 4):
        orbs.shared(d)
        take_c(other(-d))

    def add_slots(g, carry):
        products = []
        for j in range(GROUP):
            k = g * GROUP + j
            both = mm(t_cat[k], c_cat[nu_s[k]])
            products.append(both[:, :BS] + both[:, BS:])
        for j in range(GROUP):
            k = g * GROUP + j
            run[k] = products[j] + run[prev_s[k]]
        return carry

    lax.fori_loop(0, SLOTS // GROUP, add_slots, 0)

    d_cp = {}
    for off in (4, 3, 5, 2, 6, 1, 7, 0):
        d_send[off] = run[last_s[other(off)]]
        d_cp[off] = send(d_send.at[off], d_recv.at[off], d_s.at[off], d_r.at[off], partner)

    def add_core(off):
        d_cp[off].wait_recv()
        d_recv[off] = d_recv[off] + run[last_s[block(off)]]

    g_cp = {}

    def pass_on(off, part, way, kind, hop):
        rows = pl.ds(part * BS + half * way, half) if kind == 3 else pl.ds(part * BS, BS)
        n = (part * 2 + way) * 4 + kind
        g_cp[part, way, kind] = send(
            d_recv.at[off, rows], ring.at[way, kind, rows], g_s.at[n], g_r.at[n],
            ydev(hop if way == 0 else -hop),
        )

    def receive(off, part, way, kind):
        rows = pl.ds(part * BS + half * way, half) if kind == 3 else pl.ds(part * BS, BS)
        g_cp[part, way, kind].wait_recv()
        d_recv[off, rows, :] = d_recv[off, rows, :] + ring[way, kind, rows, :]

    add_core(4)
    for way in (0, 1):
        pass_on(4, 0, way, 3, 2)
    for way, off in ((0, 3), (1, 5)):
        add_core(off)
        pass_on(off, 0, way, 0, 1)
    for way, off in ((0, 3), (1, 5)):
        pass_on(4, 1, way, 3, 2)
        pass_on(off, 1, way, 0, 1)
    add_core(2)
    add_core(6)
    for part in (0, 1):
        for way, off in ((0, 2), (1, 6)):
            receive(off, part, way, 3)
            receive(off, part, way, 0)
            pass_on(off, part, way, 1, 1)
    add_core(1)
    add_core(7)
    add_core(0)
    for part in (0, 1):
        for way, off in ((0, 1), (1, 7)):
            receive(off, part, way, 1)
            pass_on(off, part, way, 2, 1)
    for d in FAR_FIRST:
        m_cp[d].wait_recv()
    mix_hi, mix_lo = split(kr_all[...].reshape(256, 256))
    mix[0] = mix_hi
    mix[1] = mix_lo

    z_cp = {}
    for part in (0, 1):
        for way in (0, 1):
            g_cp[part, way, 2].wait_recv()
        rows = pl.ds(part * BS, BS)
        ho[part] = d_recv[0, rows, :] + (ring[0, 2, rows, :] + ring[1, 2, rows, :])
        for d in FAR_FIRST:
            rows = pl.ds(pl.multiple_of(zpos(d) * 16, 16), 16)
            n = d * 2 + part
            z_cp[n] = send(ho.at[part, rows], hz.at[q, part], z_s.at[n], z_r.at[n], zdev(d))
        hz[q, part] = ho[part, pl.ds(pl.multiple_of(q * 16, 16), 16), :]
    drain(14)
    for n in sorted(z_cp):
        z_cp[n].wait_recv()
    hz_hi, hz_lo = split(hz[...].reshape(256, BS))

    fitted = mm(mix[0], hz_hi) + (mm(mix[0], hz_lo) + mm(mix[1], hz_hi))
    lb[p] = fitted
    rb[q] = fitted

    f_cp = {}
    fd_cp = {}
    rows_of = 64

    def hand_on(axis, way, part, d, kind, hop):
        sign = 1 if way == 0 else -1
        buf, ss, rs = ((lb, fy_s, fy_r), (rb, fz_s, fz_r))[axis]
        i = block(-sign * d) if axis == 0 else zpos(-sign * d)
        at = buf.at[i, pl.ds(part * rows_of, rows_of)]
        n = (part * 2 + way) * 4 + kind
        dev = ydev(sign * hop) if axis == 0 else zdev(sign * hop)
        f_cp[axis, way, part, kind] = send(at, at, ss.at[n], rs.at[n], dev)

    def to_partner(d, part):
        at = lb.at[block(-d), pl.ds(part * rows_of, rows_of)]
        n = (d % 8) * 4 + part
        fd_cp[d % 8, part] = send(at, at, fd_s.at[n], fd_r.at[n], partner)

    def put_left(i, part):
        hi, lo = split(lb[i, pl.ds(part * rows_of, rows_of), :])
        rows = pl.ds(pl.multiple_of(i * 16, 16), 16)
        for j in range(4):
            at = (part * 4 + j) * 256
            l_cat[rows, pl.ds(at, BS)] = hi[16 * j : 16 * j + 16]
            l_cat[rows, pl.ds(at + BS, BS)] = lo[16 * j : 16 * j + 16]

    def put_right(i, part):
        hi, lo = split(rb[i, pl.ds(part * rows_of, rows_of), :])
        for s, x in enumerate((hi, lo)):
            rows = pl.ds(pl.multiple_of(i * 16 + BS * s, 16), 16)
            for j in range(4):
                at = (part * 4 + j) * 256
                r_cat[rows, pl.ds(at, BS)] = x[16 * j : 16 * j + 16]
                r_cat[rows, pl.ds(at + BS, BS)] = x[16 * j : 16 * j + 16]

    def put(axis, d, part):
        if axis == 0:
            put_left(block(-d), part)
        else:
            put_right(zpos(-d), part)

    def put_shared(d, part):
        fd_cp[d % 8, part].wait_recv()
        put_left(other(-d), part)

    def piece(way, turn):
        return (turn + 2 * way) % 4

    for turn in range(4):
        for way in (0, 1):
            for axis in (0, 1):
                hand_on(axis, way, piece(way, turn), 0, 0, 1)
    for part in range(4):
        to_partner(0, part)
    for part in range(4):
        put(0, 0, part)
        put(1, 0, part)
    for turn in range(4):
        for way, sign in ((0, 1), (1, -1)):
            part = piece(way, turn)
            for axis in (0, 1):
                f_cp[axis, way, part, 0].wait_recv()
                hand_on(axis, way, part, 1, 1, 1)
            to_partner(sign, part)
    for part in range(4):
        for sign in (1, -1):
            for axis in (0, 1):
                put(axis, sign, part)
        put_shared(0, part)
    for turn in range(4):
        for way, sign in ((0, 1), (1, -1)):
            part = piece(way, turn)
            for axis in (0, 1):
                f_cp[axis, way, part, 1].wait_recv()
                if turn < 2:
                    hand_on(axis, way, part, 2, 3, 2)
                hand_on(axis, way, part, 2, 2, 1)
            to_partner(2 * sign, part)
    for part in range(4):
        for sign in (1, -1):
            put_shared(sign, part)
            for axis in (0, 1):
                put(axis, 2 * sign, part)
    for turn in range(4):
        for kind in (3, 2):
            if kind == 3 and turn >= 2:
                continue
            for way, sign in ((0, 1), (1, -1)):
                part = piece(way, turn)
                for axis in (0, 1):
                    f_cp[axis, way, part, kind].wait_recv()
                    if axis == 0:
                        to_partner((kind + 1) * sign, part)
                    put(axis, (kind + 1) * sign, part)
    for part in range(4):
        for d in (2, -2):
            put_shared(d, part)

    k_part = None
    for part in (0, 1):
        for quarter in (2 * part, 2 * part + 1):
            for d in (3, -3, 4):
                put_shared(d, quarter)
        lanes = pl.ds(part * 2048, 2048)
        both = mm(l_cat[:, lanes], r_cat[:, lanes], nt=True)
        both = both[:, :BS] + both[:, BS:]
        k_part = both if part == 0 else k_part + both
    tiles = k_part.reshape(16, 2, 8, BS)
    low = lax.broadcasted_iota(jnp.int32, (8, BS), 0) < 4
    for j in range(NX):
        for pair in range(8):
            first, second = tiles[2 * pair, j // 2], tiles[2 * pair + 1, j // 2]
            if j % 2 == 0:
                tile = jnp.where(low, first, pltpu.roll(second, 4, 0))
            else:
                tile = jnp.where(low, pltpu.roll(first, 4, 0), second)
            pk[j, pair] = tile
    x_cp = {}
    for d in (2, 1, 3):
        to = lax.rem(b + d, NX)
        x_cp[d] = send(pk.at[to], xr.at[d], x_s.at[d], x_r.at[d], xdev(d))
    drain(3)
    for d in range(1, NX):
        x_cp[d].wait_recv()
    kf[p] = (pk[b] + xr[1]) + (xr[2] + xr[3])

    cols = Gather(lambda h: kf.at[p, pl.ds(4 * h, 4)], kf.at[p], kf, 4, (k_s, k_r, kd_s, kd_r))
    cols.far(0)
    cols.far(1)
    cols.near()
    cols.relay(0)
    cols.relay(1)
    for d in (1, -1, 3, -3, 4):
        cols.take(d)
    for d in (0, 2, -2, 1, -1, 3, -3, 4):
        cols.shared(d)

    for k in range(SLOTS):
        mu = mu_s[k]
        tile = kf[nu_s[k], mu >> 1]
        rows = jnp.where(mu & 1 == 1, tile[4:8], tile[0:4])
        o_ref[k] = jnp.where(k < live, rows, jnp.zeros_like(rows))
    drain()


def per_device(three_centre, pair_mu, pair_nu, live_counts, orbitals, metric):
    hbm = pl.BlockSpec(memory_space=pltpu.HBM)

    def sems(*counts):
        return [pltpu.SemaphoreType.DMA((n,)) for n in counts for _ in range(2)]

    return pl.pallas_call(
        kernel,
        out_shape=jax.ShapeDtypeStruct((SLOTS, 4, BS), F32),
        in_specs=[hbm] * 6,
        out_specs=pl.BlockSpec(memory_space=pltpu.VMEM),
        scratch_shapes=[
            pltpu.SMEM((SLOTS,), jnp.int32),
            pltpu.SMEM((SLOTS,), jnp.int32),
            pltpu.SMEM((1,), jnp.int32),
            pltpu.SMEM((SLOTS,), jnp.int32),
            pltpu.SMEM((NB,), jnp.int32),
            pltpu.VMEM((SLOTS, 2, BS, BS), F32),
            pltpu.VMEM((SLOTS, 2 * BS, 2 * BS), BF16),
            pltpu.VMEM((SLOTS + 1, 2 * BS, BS), F32),
            pltpu.VMEM((NB, BS, BS), F32),
            pltpu.VMEM((NB, 2 * BS, 2 * BS), BF16),
            pltpu.VMEM((2, 16), F32),
            pltpu.VMEM((32, 256), F32),
            pltpu.VMEM((NZ, 32, 256), F32),
            pltpu.VMEM((2, 256, 256), BF16),
            pltpu.VMEM((NY, 2 * BS, BS), F32),
            pltpu.VMEM((NY, 2 * BS, BS), F32),
            pltpu.VMEM((2, 4, 2 * BS, BS), F32),
            pltpu.VMEM((2, BS, BS), F32),
            pltpu.VMEM((NZ, 2, 16, BS), F32),
            pltpu.VMEM((NB, 256, BS), F32),
            pltpu.VMEM((NZ, 256, BS), F32),
            pltpu.VMEM((256, 4096), BF16),
            pltpu.VMEM((256, 4096), BF16),
            pltpu.VMEM((NX, 8, 8, BS), F32),
            pltpu.VMEM((NX, 8, 8, BS), F32),
            pltpu.VMEM((NB, 8, 8, BS), F32),
            pltpu.SemaphoreType.DMA((6,)),
        ]
        + sems(12, 8, 8, 8, 16, 16, 32, 32, 32, 4, 12, 8),
        compiler_params=pltpu.CompilerParams(
            collective_id=0, has_side_effects=True, vmem_limit_bytes=56 * 2**20
        ),
        name="exchange",
    )(pair_mu, pair_nu, live_counts, three_centre, orbitals, metric)


def solution(mesh):
    in_specs = (
        P("pair", "ri", None, None),
        P("pair"),
        P("pair"),
        P("pair"),
        P("pair", "batch"),
        P("ri", None),
    )
    return jax.shard_map(
        per_device,
        mesh=mesh,
        in_specs=in_specs,
        out_specs=P("pair", ("ri", "batch"), None),
        check_vma=False,
    )
```

```python
import jax
import jax.numpy as jnp
from jax import lax
from jax.experimental import pallas as pl
from jax.experimental.pallas import tpu as pltpu
from jax.sharding import PartitionSpec as P

MESH = pl.DeviceIdType.MESH
F32 = jnp.float32
BF16 = jnp.bfloat16
SLOTS = 32
NB = 16
BS = 128
NY, NZ, NX = 8, 8, 4
GROUP = 8
FAR_FIRST = (4, 3, 5, 2, 6, 1, 7)


def split(x):
    hi = x.astype(BF16)
    return hi, (x - hi.astype(F32)).astype(BF16)


def mm(a, b, nt=False):
    dims = (((1,), (1 if nt else 0,)), ((), ()))
    return lax.dot_general(a, b, dims, preferred_element_type=F32)


def kernel(
    mu_any, nu_any, live_any, t_any, c_any, m_any, o_ref,
    mu_s, nu_s, live_s, links_s, links_v,
    t_v, t_cat, run, c_raw, c_cat, m_v, kr_own, kr_all, mix, d_send, d_recv, ring, ho, hz, lb, rb, l_cat, r_cat,
    pk, xr, kf,
    in_sem, a_s, a_r, ad_s, ad_r, m_s, m_r, d_s, d_r, g_s, g_r, z_s, z_r,
    fy_s, fy_r, fz_s, fz_r, fd_s, fd_r, x_s, x_r, k_s, k_r, kd_s, kd_r,
):
    p, q, b = lax.axis_index("pair"), lax.axis_index("ri"), lax.axis_index("batch")
    y, c = p // 2, lax.rem(p, 2)

    def ypos(d):
        return lax.rem(y + d + NY, NY)

    def ydev(d):
        return (ypos(d) * 2 + c, q, b)

    def zpos(d):
        return lax.rem(q + d + NZ, NZ)

    def zdev(d):
        return (p, zpos(d), b)

    def xdev(d):
        return (p, q, lax.rem(b + d + NX, NX))

    partner = (y * 2 + 1 - c, q, b)
    sent = []

    def send(src, dst, ss, rs, dev):
        cp = pltpu.make_async_remote_copy(
            src_ref=src, dst_ref=dst, send_sem=ss, recv_sem=rs, device_id=dev, device_id_type=MESH
        )
        cp.start()
        sent.append(cp)
        return cp

    def drain(keep=0):
        while len(sent) > keep:
            sent.pop(0).wait_send()

    def block(d):
        return ypos(d) * 2 + c

    def other(d):
        return ypos(d) * 2 + 1 - c

    class Gather:
        def __init__(self, piece, whole, buf, half, sems):
            self.piece, self.whole, self.buf, self.half, self.sems = piece, whole, buf, half, sems
            self.cp, self.dp = {}, {}

        def post(self, key, src, dst, d):
            ss, rs, _, _ = self.sems
            n = len(self.cp)
            self.cp[key] = send(src, dst, ss.at[n], rs.at[n], ydev(d))

        def at(self, i, h):
            return self.buf.at[i, pl.ds(self.half * h, self.half)]

        def far(self, turn):
            for s in (1, -1):
                h = turn if s == 1 else 1 - turn
                self.post((2 * s, h), self.piece(h), self.at(p, h), 2 * s)

        def near(self):
            for s in (1, -1):
                self.post(s, self.whole, self.buf.at[p], s)
            self.share(0, self.whole)

        def relay(self, turn):
            for s in (1, -1):
                h = turn if s == 1 else 1 - turn
                self.cp[2 * s, h].wait_recv()
                at = self.at(block(-2 * s), h)
                if turn == 0:
                    self.post(4 * s, at, at, 2 * s)
                self.post((3 * s, h), at, at, s)
            if turn == 1:
                self.share(2)
                self.share(-2)

        def share(self, d, src=None):
            _, _, ds, dr = self.sems
            at = self.buf.at[block(-d)]
            self.dp[d] = send(at if src is None else src, at, ds.at[d % 8], dr.at[d % 8], partner)

        def take(self, d):
            for key in {1: (1,), -1: (-1,), 3: ((3, 0), (3, 1)), -3: ((-3, 1), (-3, 0)), 4: (4, -4)}[d]:
                self.cp[key].wait_recv()
            self.share(d)

        def shared(self, d):
            self.dp[d].wait_recv()

    ins = [
        pltpu.make_async_copy(src, dst, in_sem.at[i])
        for i, (src, dst) in enumerate(
            ((c_any, c_raw.at[p]), (mu_any, mu_s), (nu_any, nu_s), (live_any, live_s), (m_any, m_v), (t_any, t_v))
        )
    ]
    for cp in ins:
        cp.start()
    barrier = pltpu.get_barrier_semaphore()
    peers = [ydev(d) for d in (1, -1, 2, -2)] + [zdev(d) for d in range(1, NZ)]
    peers += [xdev(d) for d in range(1, NX)] + [partner]
    for dev in peers:
        pl.semaphore_signal(barrier, inc=1, device_id=dev, device_id_type=MESH)
    pl.semaphore_wait(barrier, len(peers))

    half = BS // 2
    orbs = Gather(lambda h: c_any.at[pl.ds(half * h, half)], c_any, c_raw, half, (a_s, a_r, ad_s, ad_r))
    orbs.far(0)
    orbs.far(1)
    ins[4].wait()
    col = lax.broadcasted_iota(jnp.int32, (8, BS), 1)
    spot = (col % 8) == lax.broadcasted_iota(jnp.int32, (8, BS), 0)
    for j in range(2):
        wide = jnp.zeros((8, BS), F32)
        for i in range(16):
            wide = jnp.where((col >= 8 * i) & spot, m_v[pl.ds(j, 1), pl.ds(i, 1)], wide)
        kr_own[pl.ds(8 * j, 8), :] = wide
    kr_all[q] = kr_own[...]
    m_cp = {d: send(kr_own, kr_all.at[q], m_s.at[d], m_r.at[d], zdev(d)) for d in FAR_FIRST}
    orbs.near()

    for i in (1, 2, 3):
        ins[i].wait()
    live = live_s[0]

    lane = lax.broadcasted_iota(jnp.int32, (SLOTS, BS), 1)
    sub = lax.broadcasted_iota(jnp.int32, (SLOTS, BS), 0)
    down, across = jnp.zeros((SLOTS, BS), jnp.int32), lane - SLOTS
    for k in range(SLOTS):
        down = jnp.where(sub == k, mu_s[k], down)
        across = jnp.where(lane == k, mu_s[k], across)
    found = jnp.where((down == across) & (sub < jnp.where(lane < SLOTS, lane, live)), sub, -1)
    best = jnp.maximum(jnp.maximum(found[0:8], found[8:16]), jnp.maximum(found[16:24], found[24:32]))
    for shift in (4, 2, 1):
        best = jnp.maximum(best, pltpu.roll(best, shift, 0))
    links_v[...] = jnp.where(best < 0, SLOTS, best)
    links = pltpu.make_async_copy(links_v, links_s, in_sem.at[6])
    links.start()

    def prev_of(k):
        return links_s[0, k]

    def last_of(a):
        return links_s[0, SLOTS + a]

    def take_c(i):
        hi, lo = split(c_raw[i])
        for j in range(2):
            c_cat[i, pl.ds(BS * j, BS), pl.ds(0, BS)] = hi
            c_cat[i, pl.ds(BS * j, BS), pl.ds(BS, BS)] = lo

    def split_t(k, carry):
        for h in (0, 1):
            hi, lo = split(t_v[k, :, :, h].reshape(BS, BS))
            t_cat[k, pl.ds(BS * h, BS), pl.ds(0, BS)] = hi
            t_cat[k, pl.ds(BS * h, BS), pl.ds(BS, BS)] = lo
        return carry

    ins[5].wait()
    lax.fori_loop(0, 12, split_t, 0)
    orbs.relay(0)
    orbs.relay(1)
    for d in (1, -1):
        orbs.take(d)
    lax.fori_loop(12, SLOTS, split_t, 0)
    links.wait()
    ins[0].wait()
    take_c(p)
    for d in (2, -2, 1, -1):
        take_c(block(-d))
    for d in (0, 2, -2, 1, -1):
        orbs.shared(d)
        take_c(other(-d))
    for d in (3, -3, 4):
        orbs.take(d)
        take_c(block(-d))
    run[SLOTS] = jnp.zeros((2 * BS, BS), F32)
    for d in (3, -3, 4):
        orbs.shared(d)
        take_c(other(-d))

    def add_slots(g, carry):
        products = []
        for j in range(GROUP):
            k = g * GROUP + j
            both = mm(t_cat[k], c_cat[nu_s[k]])
            products.append(both[:, :BS] + both[:, BS:])
        for j in range(GROUP):
            k = g * GROUP + j
            run[k] = products[j] + run[prev_of(k)]
        return carry

    lax.fori_loop(0, SLOTS // GROUP, add_slots, 0)

    d_cp = {}
    for off in (4, 3, 5, 2, 6, 1, 7, 0):
        d_send[off] = run[last_of(other(off))]
        d_cp[off] = send(d_send.at[off], d_recv.at[off], d_s.at[off], d_r.at[off], partner)

    def add_core(off):
        d_cp[off].wait_recv()
        d_recv[off] = d_recv[off] + run[last_of(block(off))]

    g_cp = {}

    def pass_on(off, part, way, kind, hop):
        rows = pl.ds(part * BS + half * way, half) if kind == 3 else pl.ds(part * BS, BS)
        n = (part * 2 + way) * 4 + kind
        g_cp[part, way, kind] = send(
            d_recv.at[off, rows], ring.at[way, kind, rows], g_s.at[n], g_r.at[n],
            ydev(hop if way == 0 else -hop),
        )

    def receive(off, part, way, kind):
        rows = pl.ds(part * BS + half * way, half) if kind == 3 else pl.ds(part * BS, BS)
        g_cp[part, way, kind].wait_recv()
        d_recv[off, rows, :] = d_recv[off, rows, :] + ring[way, kind, rows, :]

    add_core(4)
    for way in (0, 1):
        pass_on(4, 0, way, 3, 2)
    for way, off in ((0, 3), (1, 5)):
        add_core(off)
        pass_on(off, 0, way, 0, 1)
    for way, off in ((0, 3), (1, 5)):
        pass_on(4, 1, way, 3, 2)
        pass_on(off, 1, way, 0, 1)
    add_core(2)
    add_core(6)
    for part in (0, 1):
        for way, off in ((0, 2), (1, 6)):
            receive(off, part, way, 3)
            receive(off, part, way, 0)
            pass_on(off, part, way, 1, 1)
    add_core(1)
    add_core(7)
    add_core(0)
    for part in (0, 1):
        for way, off in ((0, 1), (1, 7)):
            receive(off, part, way, 1)
            pass_on(off, part, way, 2, 1)
    for d in FAR_FIRST:
        m_cp[d].wait_recv()
    mix_hi, mix_lo = split(kr_all[...].reshape(BS, BS))
    mix[0] = mix_hi
    mix[1] = mix_lo

    z_cp = {}
    for h in (0, 1):
        for way in (0, 1):
            g_cp[h, way, 2].wait_recv()
        rows = pl.ds(h * BS, BS)
        total = d_recv[0, rows, :] + (ring[0, 2, rows, :] + ring[1, 2, rows, :])
        ho[h] = total.reshape(2, NZ, 8, BS)
        for d in FAR_FIRST:
            n = d * 2 + h
            z_cp[h, d] = send(ho.at[h, :, zpos(d)], hz.at[h, q], z_s.at[n], z_r.at[n], zdev(d))
        hz[h, q] = ho[h, :, pl.ds(q, 1)].reshape(2, 8, BS)
    drain(14)

    f_cp = {}
    fd_cp = {}
    ways = ((0, 1), (1, -1))

    def fit(h):
        for d in FAR_FIRST:
            z_cp[h, d].wait_recv()
        hi, lo = split(hz[h].reshape(BS, BS))
        fitted = mm(mix[0], hi) + (mm(mix[0], lo) + mm(mix[1], hi))
        lb[h, p] = fitted
        rb[q, h] = fitted

    def hand_on(axis, way, h, u, d, kind, hop):
        sign = 1 if way == 0 else -1
        rows = pl.ds(half * u, half)
        at = lb.at[h, block(-sign * d), rows] if axis == 0 else rb.at[zpos(-sign * d), h, rows]
        ss, rs = (fy_s, fy_r) if axis == 0 else (fz_s, fz_r)
        n = ((h * 2 + u) * 2 + way) * 4 + kind
        dev = ydev(sign * hop) if axis == 0 else zdev(sign * hop)
        f_cp[axis, way, h, u, kind] = send(at, at, ss.at[n], rs.at[n], dev)

    def to_partner(d, h, u):
        at = lb.at[h, block(-d), pl.ds(half * u, half)]
        n = (d % 8) * 4 + h * 2 + u
        fd_cp[d % 8, h, u] = send(at, at, fd_s.at[n], fd_r.at[n], partner)

    def first_hop(h):
        for turn in (0, 1):
            for way, sign in ways:
                for axis in (0, 1):
                    hand_on(axis, way, h, way ^ turn, 0, 0, 1)
        for u in (0, 1):
            to_partner(0, h, u)

    def next_hop(h, kind):
        for turn in (0, 1):
            for way, sign in ways:
                u = way ^ turn
                for axis in (0, 1):
                    f_cp[axis, way, h, u, kind - 1].wait_recv()
                    if kind == 2 and turn == 0:
                        hand_on(axis, way, h, u, 2, 3, 2)
                    hand_on(axis, way, h, u, kind, kind, 1)
                to_partner(kind * sign, h, u)

    def last_hop(h):
        for kind, turn in ((3, 0), (2, 0), (2, 1)):
            for way, sign in ways:
                for axis in (0, 1):
                    f_cp[axis, way, h, way ^ turn, kind].wait_recv()
                to_partner((kind + 1) * sign, h, way ^ turn)

    def put_left(h):
        for d in range(8):
            for u in (0, 1):
                fd_cp[d, h, u].wait_recv()
        rows = pl.ds(BS * h, BS)
        for j in range(16):
            hi, lo = split(lb[h, :, pl.ds(8 * j, 8), :].reshape(BS, BS))
            l_cat[rows, pl.ds(256 * j, BS)] = hi
            l_cat[rows, pl.ds(256 * j + BS, BS)] = lo

    def put_right():
        for j in range(16):
            for s, x in enumerate(split(rb[:, :, pl.ds(8 * j, 8), :].reshape(BS, BS))):
                r_cat[pl.ds(BS * s, BS), pl.ds(256 * j, BS)] = x
                r_cat[pl.ds(BS * s, BS), pl.ds(256 * j + BS, BS)] = x

    for h in (0, 1):
        fit(h)
        first_hop(h)
    for kind in (1, 2):
        for h in (0, 1):
            next_hop(h, kind)
    for h in (0, 1):
        last_hop(h)
    put_left(0)
    put_right()
    put_left(1)

    k_part = None
    for part in (0, 1):
        lanes = pl.ds(part * 2048, 2048)
        both = mm(l_cat[:, lanes], r_cat[:, lanes], nt=True)
        both = both[:, :BS] + both[:, BS:]
        k_part = both if part == 0 else k_part + both
    tiles = k_part.reshape(2, 16, 8, BS)
    low = lax.broadcasted_iota(jnp.int32, (8, BS), 0) < 4
    for j in range(NX):
        for pair in range(8):
            first, second = tiles[j // 2, 2 * pair], tiles[j // 2, 2 * pair + 1]
            if j % 2 == 0:
                tile = jnp.where(low, first, pltpu.roll(second, 4, 0))
            else:
                tile = jnp.where(low, pltpu.roll(first, 4, 0), second)
            pk[j, pair] = tile
    x_cp = {}
    for d in (2, 1, 3):
        to = lax.rem(b + d, NX)
        x_cp[d] = send(pk.at[to], xr.at[d], x_s.at[d], x_r.at[d], xdev(d))
    drain(3)
    for d in range(1, NX):
        x_cp[d].wait_recv()
    kf[p] = (pk[b] + xr[1]) + (xr[2] + xr[3])

    cols = Gather(lambda h: kf.at[p, pl.ds(4 * h, 4)], kf.at[p], kf, 4, (k_s, k_r, kd_s, kd_r))
    cols.far(0)
    cols.far(1)
    cols.near()
    cols.relay(0)
    cols.relay(1)
    for d in (1, -1, 3, -3, 4):
        cols.take(d)
    for d in (0, 2, -2, 1, -1, 3, -3, 4):
        cols.shared(d)

    for k in range(SLOTS):
        mu = mu_s[k]
        tile = kf[nu_s[k], mu >> 1]
        rows = jnp.where(mu & 1 == 1, tile[4:8], tile[0:4])
        o_ref[k] = jnp.where(k < live, rows, jnp.zeros_like(rows))
    drain()


def per_device(three_centre, pair_mu, pair_nu, live_counts, orbitals, metric):
    hbm = pl.BlockSpec(memory_space=pltpu.HBM)
    tensor = three_centre.reshape(SLOTS, 2, NZ, 2, 8, BS)

    def sems(*counts):
        return [pltpu.SemaphoreType.DMA((n,)) for n in counts for _ in range(2)]

    return pl.pallas_call(
        kernel,
        out_shape=jax.ShapeDtypeStruct((SLOTS, 4, BS), F32),
        in_specs=[hbm] * 6,
        out_specs=pl.BlockSpec(memory_space=pltpu.VMEM),
        scratch_shapes=[
            pltpu.SMEM((SLOTS,), jnp.int32),
            pltpu.SMEM((SLOTS,), jnp.int32),
            pltpu.SMEM((1,), jnp.int32),
            pltpu.SMEM((8, BS), jnp.int32),
            pltpu.VMEM((8, BS), jnp.int32),
            pltpu.VMEM((SLOTS, 2, NZ, 2, 8, BS), F32),
            pltpu.VMEM((SLOTS, 2 * BS, 2 * BS), BF16),
            pltpu.VMEM((SLOTS + 1, 2 * BS, BS), F32),
            pltpu.VMEM((NB, BS, BS), F32),
            pltpu.VMEM((NB, 2 * BS, 2 * BS), BF16),
            pltpu.VMEM((2, 16), F32),
            pltpu.VMEM((16, BS), F32),
            pltpu.VMEM((NZ, 16, BS), F32),
            pltpu.VMEM((2, BS, BS), BF16),
            pltpu.VMEM((NY, 2 * BS, BS), F32),
            pltpu.VMEM((NY, 2 * BS, BS), F32),
            pltpu.VMEM((2, 4, 2 * BS, BS), F32),
            pltpu.VMEM((2, 2, NZ, 8, BS), F32),
            pltpu.VMEM((2, NZ, 2, 8, BS), F32),
            pltpu.VMEM((2, NB, BS, BS), F32),
            pltpu.VMEM((NZ, 2, BS, BS), F32),
            pltpu.VMEM((256, 4096), BF16),
            pltpu.VMEM((256, 4096), BF16),
            pltpu.VMEM((NX, 8, 8, BS), F32),
            pltpu.VMEM((NX, 8, 8, BS), F32),
            pltpu.VMEM((NB, 8, 8, BS), F32),
            pltpu.SemaphoreType.DMA((7,)),
        ]
        + sems(12, 8, 8, 8, 16, 16, 32, 32, 32, 4, 12, 8),
        compiler_params=pltpu.CompilerParams(
            collective_id=0, has_side_effects=True, vmem_limit_bytes=56 * 2**20
        ),
        name="exchange",
    )(pair_mu, pair_nu, live_counts, tensor, orbitals, metric)


def solution(mesh):
    in_specs = (
        P("pair", "ri", None, None),
        P("pair"),
        P("pair"),
        P("pair"),
        P("pair", "batch"),
        P("ri", None),
    )
    return jax.shard_map(
        per_device,
        mesh=mesh,
        in_specs=in_specs,
        out_specs=P("pair", ("ri", "batch"), None),
        check_vma=False,
    )
```

```python
import jax
import jax.numpy as jnp
from jax import lax
from jax.experimental import pallas as pl
from jax.experimental.pallas import tpu as pltpu
from jax.sharding import PartitionSpec as P

MESH = pl.DeviceIdType.MESH
F32 = jnp.float32
BF16 = jnp.bfloat16
SLOTS = 32
NB = 16
BS = 128
NY, NZ, NX = 8, 8, 4
GROUP = 8
FAR_FIRST = (4, 3, 5, 2, 6, 1, 7)


def split(x):
    hi = x.astype(BF16)
    return hi, (x - hi.astype(F32)).astype(BF16)


def mm(a, b, nt=False):
    dims = (((1,), (1 if nt else 0,)), ((), ()))
    return lax.dot_general(a, b, dims, preferred_element_type=F32)


def kernel(
    mu_any, nu_any, live_any, t_any, c_any, m_any, o_ref,
    mu_s, nu_s, live_s, links_s, links_v,
    t_v, t_cat, run, c_raw, c_cat, m_v, kr_own, kr_all, mix, d_send, d_recv, ring, ho, hz, lb, rb, l_cat, r_cat,
    pk, xr, kf,
    in_sem, a_s, a_r, ad_s, ad_r, m_s, m_r, d_s, d_r, g_s, g_r, z_s, z_r,
    fy_s, fy_r, fz_s, fz_r, fd_s, fd_r, x_s, x_r, k_s, k_r, kd_s, kd_r,
):
    p, q, b = lax.axis_index("pair"), lax.axis_index("ri"), lax.axis_index("batch")
    y, c = p // 2, lax.rem(p, 2)

    def ypos(d):
        return lax.rem(y + d + NY, NY)

    def ydev(d):
        return (ypos(d) * 2 + c, q, b)

    def zpos(d):
        return lax.rem(q + d + NZ, NZ)

    def zdev(d):
        return (p, zpos(d), b)

    def xdev(d):
        return (p, q, lax.rem(b + d + NX, NX))

    partner = (y * 2 + 1 - c, q, b)
    sent = []

    def send(src, dst, ss, rs, dev):
        cp = pltpu.make_async_remote_copy(
            src_ref=src, dst_ref=dst, send_sem=ss, recv_sem=rs, device_id=dev, device_id_type=MESH
        )
        cp.start()
        sent.append(cp)
        return cp

    def drain(keep=0):
        while len(sent) > keep:
            sent.pop(0).wait_send()

    def block(d):
        return ypos(d) * 2 + c

    def other(d):
        return ypos(d) * 2 + 1 - c

    class Gather:
        def __init__(self, piece, whole, buf, half, sems):
            self.piece, self.whole, self.buf, self.half, self.sems = piece, whole, buf, half, sems
            self.cp, self.dp = {}, {}

        def post(self, key, src, dst, d):
            ss, rs, _, _ = self.sems
            n = len(self.cp)
            self.cp[key] = send(src, dst, ss.at[n], rs.at[n], ydev(d))

        def at(self, i, h):
            return self.buf.at[i, pl.ds(self.half * h, self.half)]

        def far(self, turn):
            for s in (1, -1):
                h = turn if s == 1 else 1 - turn
                self.post((2 * s, h), self.piece(h), self.at(p, h), 2 * s)

        def near(self):
            for s in (1, -1):
                self.post(s, self.whole, self.buf.at[p], s)
            self.share(0, self.whole)

        def relay(self, turn):
            for s in (1, -1):
                h = turn if s == 1 else 1 - turn
                self.cp[2 * s, h].wait_recv()
                at = self.at(block(-2 * s), h)
                if turn == 0:
                    self.post(4 * s, at, at, 2 * s)
                self.post((3 * s, h), at, at, s)
            if turn == 1:
                self.share(2)
                self.share(-2)

        def share(self, d, src=None):
            _, _, ds, dr = self.sems
            at = self.buf.at[block(-d)]
            self.dp[d] = send(at if src is None else src, at, ds.at[d % 8], dr.at[d % 8], partner)

        def take(self, d):
            for key in {1: (1,), -1: (-1,), 3: ((3, 0), (3, 1)), -3: ((-3, 1), (-3, 0)), 4: (4, -4)}[d]:
                self.cp[key].wait_recv()
            self.share(d)

        def shared(self, d):
            self.dp[d].wait_recv()

    ins = [
        pltpu.make_async_copy(src, dst, in_sem.at[i])
        for i, (src, dst) in enumerate(
            ((c_any, c_raw.at[p]), (mu_any, mu_s), (nu_any, nu_s), (live_any, live_s), (m_any, m_v), (t_any, t_v))
        )
    ]
    for cp in ins:
        cp.start()
    barrier = pltpu.get_barrier_semaphore()
    peers = [ydev(d) for d in (1, -1, 2, -2)] + [zdev(d) for d in range(1, NZ)]
    peers += [xdev(d) for d in range(1, NX)] + [partner]
    for dev in peers:
        pl.semaphore_signal(barrier, inc=1, device_id=dev, device_id_type=MESH)
    pl.semaphore_wait(barrier, len(peers))

    half = BS // 2
    orbs = Gather(lambda h: c_any.at[pl.ds(half * h, half)], c_any, c_raw, half, (a_s, a_r, ad_s, ad_r))
    orbs.far(0)
    orbs.far(1)
    ins[4].wait()
    col = lax.broadcasted_iota(jnp.int32, (8, BS), 1)
    spot = (col % 8) == lax.broadcasted_iota(jnp.int32, (8, BS), 0)
    for j in range(2):
        wide = jnp.zeros((8, BS), F32)
        for i in range(16):
            wide = jnp.where((col >= 8 * i) & spot, m_v[pl.ds(j, 1), pl.ds(i, 1)], wide)
        kr_own[pl.ds(8 * j, 8), :] = wide
    kr_all[q] = kr_own[...]
    m_cp = {d: send(kr_own, kr_all.at[q], m_s.at[d], m_r.at[d], zdev(d)) for d in FAR_FIRST}
    orbs.near()

    for i in (1, 2, 3):
        ins[i].wait()
    live = live_s[0]

    lane = lax.broadcasted_iota(jnp.int32, (SLOTS, BS), 1)
    sub = lax.broadcasted_iota(jnp.int32, (SLOTS, BS), 0)
    down, across = jnp.zeros((SLOTS, BS), jnp.int32), lane - SLOTS
    for k in range(SLOTS):
        down = jnp.where(sub == k, mu_s[k], down)
        across = jnp.where(lane == k, mu_s[k], across)
    found = jnp.where((down == across) & (sub < jnp.where(lane < SLOTS, lane, live)), sub, -1)
    best = jnp.maximum(jnp.maximum(found[0:8], found[8:16]), jnp.maximum(found[16:24], found[24:32]))
    for shift in (4, 2, 1):
        best = jnp.maximum(best, pltpu.roll(best, shift, 0))
    links_v[...] = jnp.where(best < 0, SLOTS, best)
    links = pltpu.make_async_copy(links_v, links_s, in_sem.at[6])
    links.start()

    def prev_of(k):
        return links_s[0, k]

    def last_of(a):
        return links_s[0, SLOTS + a]

    def take_c(i):
        hi, lo = split(c_raw[i])
        for j in range(2):
            c_cat[i, pl.ds(BS * j, BS), pl.ds(0, BS)] = hi
            c_cat[i, pl.ds(BS * j, BS), pl.ds(BS, BS)] = lo

    def split_t(k, carry):
        for h in (0, 1):
            hi, lo = split(t_v[k, :, :, h].reshape(BS, BS))
            t_cat[k, pl.ds(BS * h, BS), pl.ds(0, BS)] = hi
            t_cat[k, pl.ds(BS * h, BS), pl.ds(BS, BS)] = lo
        return carry

    ins[5].wait()
    lax.fori_loop(0, 12, split_t, 0)
    orbs.relay(0)
    orbs.relay(1)
    for d in (1, -1):
        orbs.take(d)
    lax.fori_loop(12, SLOTS, split_t, 0)
    links.wait()
    ins[0].wait()
    take_c(p)
    for d in (2, -2, 1, -1):
        take_c(block(-d))
    for d in (0, 2, -2, 1, -1):
        orbs.shared(d)
        take_c(other(-d))
    for d in (3, -3, 4):
        orbs.take(d)
        take_c(block(-d))
    run[SLOTS] = jnp.zeros((2 * BS, BS), F32)
    for d in (3, -3, 4):
        orbs.shared(d)
        take_c(other(-d))

    def add_slots(g, carry):
        products = []
        for j in range(GROUP):
            k = g * GROUP + j
            both = mm(t_cat[k], c_cat[nu_s[k]])
            products.append(both[:, :BS] + both[:, BS:])
        for j in range(GROUP):
            k = g * GROUP + j
            run[k] = products[j] + run[prev_of(k)]
        return carry

    lax.fori_loop(0, SLOTS // GROUP, add_slots, 0)

    d_cp = {}
    for off in (4, 3, 5, 2, 6, 1, 7, 0):
        d_send[off] = run[last_of(other(off))]
        d_cp[off] = send(d_send.at[off], d_recv.at[off], d_s.at[off], d_r.at[off], partner)

    def add_core(off):
        d_cp[off].wait_recv()
        d_recv[off] = d_recv[off] + run[last_of(block(off))]

    g_cp = {}

    def pass_on(off, part, way, kind, hop):
        rows = pl.ds(part * BS + half * way, half) if kind == 3 else pl.ds(part * BS, BS)
        n = (part * 2 + way) * 4 + kind
        g_cp[part, way, kind] = send(
            d_recv.at[off, rows], ring.at[way, kind, rows], g_s.at[n], g_r.at[n],
            ydev(hop if way == 0 else -hop),
        )

    def receive(off, part, way, kind):
        rows = pl.ds(part * BS + half * way, half) if kind == 3 else pl.ds(part * BS, BS)
        g_cp[part, way, kind].wait_recv()
        d_recv[off, rows, :] = d_recv[off, rows, :] + ring[way, kind, rows, :]

    add_core(4)
    for way in (0, 1):
        pass_on(4, 0, way, 3, 2)
    for way, off in ((0, 3), (1, 5)):
        add_core(off)
        pass_on(off, 0, way, 0, 1)
    for way, off in ((0, 3), (1, 5)):
        pass_on(4, 1, way, 3, 2)
        pass_on(off, 1, way, 0, 1)
    add_core(2)
    add_core(6)
    for part in (0, 1):
        for way, off in ((0, 2), (1, 6)):
            receive(off, part, way, 3)
            receive(off, part, way, 0)
            pass_on(off, part, way, 1, 1)
    add_core(1)
    add_core(7)
    add_core(0)
    for part in (0, 1):
        for way, off in ((0, 1), (1, 7)):
            receive(off, part, way, 1)
            pass_on(off, part, way, 2, 1)
    for d in FAR_FIRST:
        m_cp[d].wait_recv()
    mix_hi, mix_lo = split(kr_all[...].reshape(BS, BS))
    mix[0] = mix_hi
    mix[1] = mix_lo

    z_cp = {}
    for h in (0, 1):
        for way in (0, 1):
            g_cp[h, way, 2].wait_recv()
        rows = pl.ds(h * BS, BS)
        total = d_recv[0, rows, :] + (ring[0, 2, rows, :] + ring[1, 2, rows, :])
        ho[h] = total.reshape(2, NZ, 8, BS)
        for d in FAR_FIRST:
            n = d * 2 + h
            z_cp[h, d] = send(ho.at[h, :, zpos(d)], hz.at[h, q], z_s.at[n], z_r.at[n], zdev(d))
        hz[h, q] = ho[h, :, pl.ds(q, 1)].reshape(2, 8, BS)
    drain(14)

    f_cp = {}
    fd_cp = {}
    ways = ((0, 1), (1, -1))

    def fit(h):
        for d in FAR_FIRST:
            z_cp[h, d].wait_recv()
        hi, lo = split(hz[h].reshape(BS, BS))
        fitted = mm(mix[0], hi) + (mm(mix[0], lo) + mm(mix[1], hi))
        lb[h, p] = fitted
        rb[q, h] = fitted

    def hand_on(axis, way, h, u, d, kind, hop):
        sign = 1 if way == 0 else -1
        rows = pl.ds(half * u, half)
        at = lb.at[h, block(-sign * d), rows] if axis == 0 else rb.at[zpos(-sign * d), h, rows]
        ss, rs = (fy_s, fy_r) if axis == 0 else (fz_s, fz_r)
        n = ((h * 2 + u) * 2 + way) * 4 + kind
        dev = ydev(sign * hop) if axis == 0 else zdev(sign * hop)
        f_cp[axis, way, h, u, kind] = send(at, at, ss.at[n], rs.at[n], dev)

    def to_partner(d, h, u):
        at = lb.at[h, block(-d), pl.ds(half * u, half)]
        n = (d % 8) * 4 + h * 2 + u
        fd_cp[d % 8, h, u] = send(at, at, fd_s.at[n], fd_r.at[n], partner)

    def first_hop(h):
        for turn in (0, 1):
            for way, sign in ways:
                for axis in (0, 1):
                    hand_on(axis, way, h, way ^ turn, 0, 0, 1)
        for u in (0, 1):
            to_partner(0, h, u)

    def next_hop(h, kind):
        for turn in (0, 1):
            for way, sign in ways:
                u = way ^ turn
                for axis in (0, 1):
                    f_cp[axis, way, h, u, kind - 1].wait_recv()
                    if kind == 2 and turn == 0:
                        hand_on(axis, way, h, u, 2, 3, 2)
                    hand_on(axis, way, h, u, kind, kind, 1)
                to_partner(kind * sign, h, u)

    def last_hop(h):
        for kind, turn in ((3, 0), (2, 0), (2, 1)):
            for way, sign in ways:
                for axis in (0, 1):
                    f_cp[axis, way, h, way ^ turn, kind].wait_recv()
                to_partner((kind + 1) * sign, h, way ^ turn)

    def put_left(h):
        for d in range(8):
            for u in (0, 1):
                fd_cp[d, h, u].wait_recv()
        rows = pl.ds(BS * h, BS)
        for j in range(16):
            hi, lo = split(lb[h, :, pl.ds(8 * j, 8), :].reshape(BS, BS))
            l_cat[rows, pl.ds(256 * j, BS)] = hi
            l_cat[rows, pl.ds(256 * j + BS, BS)] = lo

    def put_right():
        for j in range(16):
            for s, x in enumerate(split(rb[:, :, pl.ds(8 * j, 8), :].reshape(BS, BS))):
                r_cat[pl.ds(BS * s, BS), pl.ds(256 * j, BS)] = x
                r_cat[pl.ds(BS * s, BS), pl.ds(256 * j + BS, BS)] = x

    for h in (0, 1):
        fit(h)
        first_hop(h)
    for kind in (1, 2):
        for h in (0, 1):
            next_hop(h, kind)
    for h in (0, 1):
        last_hop(h)

    low = lax.broadcasted_iota(jnp.int32, (8, BS), 0) < 4

    def x_copy(j, d, dev):
        return pltpu.make_async_remote_copy(
            src_ref=pk.at[j], dst_ref=xr.at[d], send_sem=x_s.at[d], recv_sem=x_r.at[d], device_id=dev, device_id_type=MESH
        )

    def exchange(h):
        both = mm(l_cat[pl.ds(BS * h, BS), :], r_cat[...], nt=True)
        tiles = (both[:, :BS] + both[:, BS:]).reshape(16, 8, BS)
        for j in (2 * h, 2 * h + 1):
            for pair in range(8):
                first, second = tiles[2 * pair], tiles[2 * pair + 1]
                if j % 2 == 0:
                    tile = jnp.where(low, first, pltpu.roll(second, 4, 0))
                else:
                    tile = jnp.where(low, pltpu.roll(first, 4, 0), second)
                pk[j, pair] = tile

            @pl.when(b != j)
            def _():
                x_copy(j, lax.rem(j - b + NX, NX), (p, q, jnp.int32(j))).start()

    put_left(0)
    put_right()
    exchange(0)
    put_left(1)
    exchange(1)
    drain()
    for d in range(1, NX):
        x_copy(0, d, xdev(d)).wait_recv()
    kf[p] = (pk[b] + xr[1]) + (xr[2] + xr[3])

    cols = Gather(lambda h: kf.at[p, pl.ds(4 * h, 4)], kf.at[p], kf, 4, (k_s, k_r, kd_s, kd_r))
    cols.far(0)
    cols.far(1)
    cols.near()
    cols.relay(0)
    cols.relay(1)
    for d in (1, -1, 3, -3, 4):
        cols.take(d)
    for d in (0, 2, -2, 1, -1, 3, -3, 4):
        cols.shared(d)

    for k in range(SLOTS):
        mu = mu_s[k]
        tile = kf[nu_s[k], mu >> 1]
        rows = jnp.where(mu & 1 == 1, tile[4:8], tile[0:4])
        o_ref[k] = jnp.where(k < live, rows, jnp.zeros_like(rows))
    for d in range(1, NX):
        x_copy(0, d, xdev(d)).wait_send()
    drain()


def per_device(three_centre, pair_mu, pair_nu, live_counts, orbitals, metric):
    hbm = pl.BlockSpec(memory_space=pltpu.HBM)
    tensor = three_centre.reshape(SLOTS, 2, NZ, 2, 8, BS)

    def sems(*counts):
        return [pltpu.SemaphoreType.DMA((n,)) for n in counts for _ in range(2)]

    return pl.pallas_call(
        kernel,
        out_shape=jax.ShapeDtypeStruct((SLOTS, 4, BS), F32),
        in_specs=[hbm] * 6,
        out_specs=pl.BlockSpec(memory_space=pltpu.VMEM),
        scratch_shapes=[
            pltpu.SMEM((SLOTS,), jnp.int32),
            pltpu.SMEM((SLOTS,), jnp.int32),
            pltpu.SMEM((1,), jnp.int32),
            pltpu.SMEM((8, BS), jnp.int32),
            pltpu.VMEM((8, BS), jnp.int32),
            pltpu.VMEM((SLOTS, 2, NZ, 2, 8, BS), F32),
            pltpu.VMEM((SLOTS, 2 * BS, 2 * BS), BF16),
            pltpu.VMEM((SLOTS + 1, 2 * BS, BS), F32),
            pltpu.VMEM((NB, BS, BS), F32),
            pltpu.VMEM((NB, 2 * BS, 2 * BS), BF16),
            pltpu.VMEM((2, 16), F32),
            pltpu.VMEM((16, BS), F32),
            pltpu.VMEM((NZ, 16, BS), F32),
            pltpu.VMEM((2, BS, BS), BF16),
            pltpu.VMEM((NY, 2 * BS, BS), F32),
            pltpu.VMEM((NY, 2 * BS, BS), F32),
            pltpu.VMEM((2, 4, 2 * BS, BS), F32),
            pltpu.VMEM((2, 2, NZ, 8, BS), F32),
            pltpu.VMEM((2, NZ, 2, 8, BS), F32),
            pltpu.VMEM((2, NB, BS, BS), F32),
            pltpu.VMEM((NZ, 2, BS, BS), F32),
            pltpu.VMEM((256, 4096), BF16),
            pltpu.VMEM((256, 4096), BF16),
            pltpu.VMEM((NX, 8, 8, BS), F32),
            pltpu.VMEM((NX, 8, 8, BS), F32),
            pltpu.VMEM((NB, 8, 8, BS), F32),
            pltpu.SemaphoreType.DMA((7,)),
        ]
        + sems(12, 8, 8, 8, 16, 16, 32, 32, 32, 4, 12, 8),
        compiler_params=pltpu.CompilerParams(
            collective_id=0, has_side_effects=True, vmem_limit_bytes=56 * 2**20
        ),
        name="exchange",
    )(pair_mu, pair_nu, live_counts, tensor, orbitals, metric)


def solution(mesh):
    in_specs = (
        P("pair", "ri", None, None),
        P("pair"),
        P("pair"),
        P("pair"),
        P("pair", "batch"),
        P("ri", None),
    )
    return jax.shard_map(
        per_device,
        mesh=mesh,
        in_specs=in_specs,
        out_specs=P("pair", ("ri", "batch"), None),
        check_vma=False,
    )
```

```python
import jax
import jax.numpy as jnp
from jax import lax
from jax.experimental import pallas as pl
from jax.experimental.pallas import tpu as pltpu
from jax.sharding import PartitionSpec as P

MESH = pl.DeviceIdType.MESH
F32 = jnp.float32
BF16 = jnp.bfloat16
SLOTS = 32
NB = 16
BS = 128
NY, NZ, NX = 8, 8, 4
GROUP = 8
FAR_FIRST = (4, 3, 5, 2, 6, 1, 7)


def split(x):
    hi = x.astype(BF16)
    return hi, (x - hi.astype(F32)).astype(BF16)


def mm(a, b, nt=False):
    dims = (((1,), (1 if nt else 0,)), ((), ()))
    return lax.dot_general(a, b, dims, preferred_element_type=F32)


def kernel(
    mu_any, nu_any, live_any, t_any, c_any, m_any, o_ref,
    mu_s, nu_s, live_s, links_s, links_v,
    t_v, t_cat, run, c_raw, c_cat, m_v, kr_own, kr_all, mix, d_send, d_recv, ring, ho, hz, lb, rb, l_cat, r_cat,
    pk, xr, kf,
    in_sem, a_s, a_r, ad_s, ad_r, m_s, m_r, d_s, d_r, g_s, g_r, z_s, z_r,
    fy_s, fy_r, fz_s, fz_r, fd_s, fd_r, x_s, x_r, k_s, k_r, kd_s, kd_r,
):
    p, q, b = lax.axis_index("pair"), lax.axis_index("ri"), lax.axis_index("batch")
    y, c = p // 2, lax.rem(p, 2)

    def ypos(d):
        return lax.rem(y + d + NY, NY)

    def ydev(d):
        return (ypos(d) * 2 + c, q, b)

    def zpos(d):
        return lax.rem(q + d + NZ, NZ)

    def zdev(d):
        return (p, zpos(d), b)

    def xdev(d):
        return (p, q, lax.rem(b + d + NX, NX))

    partner = (y * 2 + 1 - c, q, b)
    sent = []

    def send(src, dst, ss, rs, dev):
        cp = pltpu.make_async_remote_copy(
            src_ref=src, dst_ref=dst, send_sem=ss, recv_sem=rs, device_id=dev, device_id_type=MESH
        )
        cp.start()
        sent.append(cp)
        return cp

    def drain(keep=0):
        while len(sent) > keep:
            sent.pop(0).wait_send()

    def block(d):
        return ypos(d) * 2 + c

    def other(d):
        return ypos(d) * 2 + 1 - c

    class Gather:
        def __init__(self, piece, whole, buf, half, sems):
            self.piece, self.whole, self.buf, self.half, self.sems = piece, whole, buf, half, sems
            self.cp, self.dp = {}, {}

        def post(self, key, src, dst, d):
            ss, rs, _, _ = self.sems
            n = len(self.cp)
            self.cp[key] = send(src, dst, ss.at[n], rs.at[n], ydev(d))

        def at(self, i, h):
            return self.buf.at[i, pl.ds(self.half * h, self.half)]

        def far(self, turn):
            for s in (1, -1):
                h = turn if s == 1 else 1 - turn
                self.post((2 * s, h), self.piece(h), self.at(p, h), 2 * s)

        def near(self):
            for s in (1, -1):
                self.post(s, self.whole, self.buf.at[p], s)
            self.share(0, self.whole)

        def relay(self, turn):
            for s in (1, -1):
                h = turn if s == 1 else 1 - turn
                self.cp[2 * s, h].wait_recv()
                at = self.at(block(-2 * s), h)
                if turn == 0:
                    self.post(4 * s, at, at, 2 * s)
                self.post((3 * s, h), at, at, s)
            if turn == 1:
                self.share(2)
                self.share(-2)

        def share(self, d, src=None):
            _, _, ds, dr = self.sems
            at = self.buf.at[block(-d)]
            self.dp[d] = send(at if src is None else src, at, ds.at[d % 8], dr.at[d % 8], partner)

        def take(self, d):
            for key in {1: (1,), -1: (-1,), 3: ((3, 0), (3, 1)), -3: ((-3, 1), (-3, 0)), 4: (4, -4)}[d]:
                self.cp[key].wait_recv()
            self.share(d)

        def shared(self, d):
            self.dp[d].wait_recv()

    ins = [
        pltpu.make_async_copy(src, dst, in_sem.at[i])
        for i, (src, dst) in enumerate(
            ((c_any, c_raw.at[p]), (mu_any, mu_s), (nu_any, nu_s), (live_any, live_s), (m_any, m_v), (t_any, t_v))
        )
    ]
    for cp in ins:
        cp.start()
    barrier = pltpu.get_barrier_semaphore()
    peers = [ydev(d) for d in (1, -1, 2, -2)] + [zdev(d) for d in range(1, NZ)]
    peers += [xdev(d) for d in range(1, NX)] + [partner]
    for dev in peers:
        pl.semaphore_signal(barrier, inc=1, device_id=dev, device_id_type=MESH)
    pl.semaphore_wait(barrier, len(peers))

    half = BS // 2
    orbs = Gather(lambda h: c_any.at[pl.ds(half * h, half)], c_any, c_raw, half, (a_s, a_r, ad_s, ad_r))
    orbs.far(0)
    orbs.far(1)
    ins[4].wait()
    col = lax.broadcasted_iota(jnp.int32, (8, BS), 1)
    spot = (col % 8) == lax.broadcasted_iota(jnp.int32, (8, BS), 0)
    for j in range(2):
        wide = jnp.zeros((8, BS), F32)
        for i in range(16):
            wide = jnp.where((col >= 8 * i) & spot, m_v[pl.ds(j, 1), pl.ds(i, 1)], wide)
        kr_own[pl.ds(8 * j, 8), :] = wide
    kr_all[q] = kr_own[...]
    m_cp = {d: send(kr_own, kr_all.at[q], m_s.at[d], m_r.at[d], zdev(d)) for d in FAR_FIRST}
    orbs.near()

    for i in (1, 2, 3):
        ins[i].wait()
    live = live_s[0]

    lane = lax.broadcasted_iota(jnp.int32, (SLOTS, BS), 1)
    sub = lax.broadcasted_iota(jnp.int32, (SLOTS, BS), 0)
    down, across = jnp.zeros((SLOTS, BS), jnp.int32), lane - SLOTS
    for k in range(SLOTS):
        down = jnp.where(sub == k, mu_s[k], down)
        across = jnp.where(lane == k, mu_s[k], across)
    found = jnp.where((down == across) & (sub < jnp.where(lane < SLOTS, lane, live)), sub, -1)
    best = jnp.maximum(jnp.maximum(found[0:8], found[8:16]), jnp.maximum(found[16:24], found[24:32]))
    for shift in (4, 2, 1):
        best = jnp.maximum(best, pltpu.roll(best, shift, 0))
    links_v[...] = jnp.where(best < 0, SLOTS, best)
    links = pltpu.make_async_copy(links_v, links_s, in_sem.at[6])
    links.start()

    def prev_of(k):
        return links_s[0, k]

    def last_of(a):
        return links_s[0, SLOTS + a]

    def take_c(i):
        hi, lo = split(c_raw[i])
        for j in range(2):
            c_cat[i, pl.ds(BS * j, BS), pl.ds(0, BS)] = hi
            c_cat[i, pl.ds(BS * j, BS), pl.ds(BS, BS)] = lo

    def split_t(k, carry):
        for h in (0, 1):
            hi, lo = split(t_v[k, :, :, h].reshape(BS, BS))
            t_cat[k, pl.ds(BS * h, BS), pl.ds(0, BS)] = hi
            t_cat[k, pl.ds(BS * h, BS), pl.ds(BS, BS)] = lo
        return carry

    ins[5].wait()
    lax.fori_loop(0, 12, split_t, 0)
    orbs.relay(0)
    orbs.relay(1)
    for d in (1, -1):
        orbs.take(d)
    lax.fori_loop(12, SLOTS, split_t, 0)
    links.wait()
    ins[0].wait()
    take_c(p)
    for d in (2, -2, 1, -1):
        take_c(block(-d))
    for d in (0, 2, -2, 1, -1):
        orbs.shared(d)
        take_c(other(-d))
    for d in (3, -3, 4):
        orbs.take(d)
        take_c(block(-d))
    for h in (0, 1):
        run[h, SLOTS] = jnp.zeros((BS, BS), F32)
    for d in (3, -3, 4):
        orbs.shared(d)
        take_c(other(-d))

    d_cp = {}

    def half_transform(h):
        rows = pl.ds(BS * h, BS)

        def add_slots(g, carry):
            products = []
            for j in range(GROUP):
                k = g * GROUP + j
                both = mm(t_cat[k, rows, :], c_cat[nu_s[k]])
                products.append(both[:, :BS] + both[:, BS:])
            for j in range(GROUP):
                k = g * GROUP + j
                run[h, k] = products[j] + run[h, prev_of(k)]
            return carry

        lax.fori_loop(0, SLOTS // GROUP, add_slots, 0)

    def swap_cores(h):
        rows = pl.ds(BS * h, BS)
        for off in (4, 3, 5, 2, 6, 1, 7, 0):
            n = off * 2 + h
            d_send[off, rows, :] = run[h, last_of(other(off))]
            d_cp[off, h] = send(d_send.at[off, rows], d_recv.at[off, rows], d_s.at[n], d_r.at[n], partner)

    def add_core(off, h):
        rows = pl.ds(BS * h, BS)
        d_cp[off, h].wait_recv()
        d_recv[off, rows, :] = d_recv[off, rows, :] + run[h, last_of(block(off))]

    g_cp = {}

    def pass_on(off, part, way, kind, hop):
        rows = pl.ds(part * BS + half * way, half) if kind == 3 else pl.ds(part * BS, BS)
        n = (part * 2 + way) * 4 + kind
        g_cp[part, way, kind] = send(
            d_recv.at[off, rows], ring.at[way, kind, rows], g_s.at[n], g_r.at[n],
            ydev(hop if way == 0 else -hop),
        )

    def receive(off, part, way, kind):
        rows = pl.ds(part * BS + half * way, half) if kind == 3 else pl.ds(part * BS, BS)
        g_cp[part, way, kind].wait_recv()
        d_recv[off, rows, :] = d_recv[off, rows, :] + ring[way, kind, rows, :]

    def first_step(h):
        add_core(4, h)
        for way in (0, 1):
            pass_on(4, h, way, 3, 2)
        for way, off in ((0, 3), (1, 5)):
            add_core(off, h)
            pass_on(off, h, way, 0, 1)

    half_transform(0)
    swap_cores(0)
    half_transform(1)
    first_step(0)
    swap_cores(1)
    for off in (2, 6, 1, 7, 0):
        add_core(off, 0)
    first_step(1)
    for off in (2, 6):
        add_core(off, 1)
    for part in (0, 1):
        for way, off in ((0, 2), (1, 6)):
            receive(off, part, way, 3)
            receive(off, part, way, 0)
            pass_on(off, part, way, 1, 1)
    for off in (1, 7, 0):
        add_core(off, 1)
    for part in (0, 1):
        for way, off in ((0, 1), (1, 7)):
            receive(off, part, way, 1)
            pass_on(off, part, way, 2, 1)
    for d in FAR_FIRST:
        m_cp[d].wait_recv()
    mix_hi, mix_lo = split(kr_all[...].reshape(BS, BS))
    mix[0] = mix_hi
    mix[1] = mix_lo

    z_cp = {}
    for h in (0, 1):
        for way in (0, 1):
            g_cp[h, way, 2].wait_recv()
        rows = pl.ds(h * BS, BS)
        total = d_recv[0, rows, :] + (ring[0, 2, rows, :] + ring[1, 2, rows, :])
        ho[h] = total.reshape(2, NZ, 8, BS)
        for d in FAR_FIRST:
            n = d * 2 + h
            z_cp[h, d] = send(ho.at[h, :, zpos(d)], hz.at[h, q], z_s.at[n], z_r.at[n], zdev(d))
        hz[h, q] = ho[h, :, pl.ds(q, 1)].reshape(2, 8, BS)
    drain(14)

    f_cp = {}
    fd_cp = {}
    ways = ((0, 1), (1, -1))

    def fit(h):
        for d in FAR_FIRST:
            z_cp[h, d].wait_recv()
        hi, lo = split(hz[h].reshape(BS, BS))
        fitted = mm(mix[0], hi) + (mm(mix[0], lo) + mm(mix[1], hi))
        lb[h, p] = fitted
        rb[q, h] = fitted

    def hand_on(axis, way, h, u, d, kind, hop):
        sign = 1 if way == 0 else -1
        rows = pl.ds(half * u, half)
        at = lb.at[h, block(-sign * d), rows] if axis == 0 else rb.at[zpos(-sign * d), h, rows]
        ss, rs = (fy_s, fy_r) if axis == 0 else (fz_s, fz_r)
        n = ((h * 2 + u) * 2 + way) * 4 + kind
        dev = ydev(sign * hop) if axis == 0 else zdev(sign * hop)
        f_cp[axis, way, h, u, kind] = send(at, at, ss.at[n], rs.at[n], dev)

    def to_partner(d, h, u):
        at = lb.at[h, block(-d), pl.ds(half * u, half)]
        n = (d % 8) * 4 + h * 2 + u
        fd_cp[d % 8, h, u] = send(at, at, fd_s.at[n], fd_r.at[n], partner)

    def first_hop(h):
        for turn in (0, 1):
            for way, sign in ways:
                for axis in (0, 1):
                    hand_on(axis, way, h, way ^ turn, 0, 0, 1)
        for u in (0, 1):
            to_partner(0, h, u)

    def next_hop(h, kind):
        for turn in (0, 1):
            for way, sign in ways:
                u = way ^ turn
                for axis in (0, 1):
                    f_cp[axis, way, h, u, kind - 1].wait_recv()
                    if kind == 2 and turn == 0:
                        hand_on(axis, way, h, u, 2, 3, 2)
                    hand_on(axis, way, h, u, kind, kind, 1)
                to_partner(kind * sign, h, u)

    def last_hop(h):
        for kind, turn in ((3, 0), (2, 0), (2, 1)):
            for way, sign in ways:
                for axis in (0, 1):
                    f_cp[axis, way, h, way ^ turn, kind].wait_recv()
                to_partner((kind + 1) * sign, h, way ^ turn)

    def put_left(h):
        for d in range(8):
            for u in (0, 1):
                fd_cp[d, h, u].wait_recv()
        rows = pl.ds(BS * h, BS)
        for j in range(16):
            hi, lo = split(lb[h, :, pl.ds(8 * j, 8), :].reshape(BS, BS))
            l_cat[rows, pl.ds(256 * j, BS)] = hi
            l_cat[rows, pl.ds(256 * j + BS, BS)] = lo

    def put_right():
        for j in range(16):
            for s, x in enumerate(split(rb[:, :, pl.ds(8 * j, 8), :].reshape(BS, BS))):
                r_cat[pl.ds(BS * s, BS), pl.ds(256 * j, BS)] = x
                r_cat[pl.ds(BS * s, BS), pl.ds(256 * j + BS, BS)] = x

    for h in (0, 1):
        fit(h)
        first_hop(h)
    for kind in (1, 2):
        for h in (0, 1):
            next_hop(h, kind)
    for h in (0, 1):
        last_hop(h)

    low = lax.broadcasted_iota(jnp.int32, (8, BS), 0) < 4

    def x_copy(j, d, dev):
        return pltpu.make_async_remote_copy(
            src_ref=pk.at[j], dst_ref=xr.at[d], send_sem=x_s.at[d], recv_sem=x_r.at[d], device_id=dev, device_id_type=MESH
        )

    def exchange(h):
        both = mm(l_cat[pl.ds(BS * h, BS), :], r_cat[...], nt=True)
        tiles = (both[:, :BS] + both[:, BS:]).reshape(16, 8, BS)
        for j in (2 * h, 2 * h + 1):
            for pair in range(8):
                first, second = tiles[2 * pair], tiles[2 * pair + 1]
                if j % 2 == 0:
                    tile = jnp.where(low, first, pltpu.roll(second, 4, 0))
                else:
                    tile = jnp.where(low, pltpu.roll(first, 4, 0), second)
                pk[j, pair] = tile

            @pl.when(b != j)
            def _():
                x_copy(j, lax.rem(j - b + NX, NX), (p, q, jnp.int32(j))).start()

    put_left(0)
    put_right()
    exchange(0)
    put_left(1)
    exchange(1)
    drain()
    for d in range(1, NX):
        x_copy(0, d, xdev(d)).wait_recv()
    kf[p] = (pk[b] + xr[1]) + (xr[2] + xr[3])

    cols = Gather(lambda h: kf.at[p, pl.ds(4 * h, 4)], kf.at[p], kf, 4, (k_s, k_r, kd_s, kd_r))
    cols.far(0)
    cols.far(1)
    cols.near()
    cols.relay(0)
    cols.relay(1)
    for d in (1, -1, 3, -3, 4):
        cols.take(d)
    for d in (0, 2, -2, 1, -1, 3, -3, 4):
        cols.shared(d)

    for k in range(SLOTS):
        mu = mu_s[k]
        tile = kf[nu_s[k], mu >> 1]
        rows = jnp.where(mu & 1 == 1, tile[4:8], tile[0:4])
        o_ref[k] = jnp.where(k < live, rows, jnp.zeros_like(rows))
    for d in range(1, NX):
        x_copy(0, d, xdev(d)).wait_send()
    drain()


def per_device(three_centre, pair_mu, pair_nu, live_counts, orbitals, metric):
    hbm = pl.BlockSpec(memory_space=pltpu.HBM)
    tensor = three_centre.reshape(SLOTS, 2, NZ, 2, 8, BS)

    def sems(*counts):
        return [pltpu.SemaphoreType.DMA((n,)) for n in counts for _ in range(2)]

    return pl.pallas_call(
        kernel,
        out_shape=jax.ShapeDtypeStruct((SLOTS, 4, BS), F32),
        in_specs=[hbm] * 6,
        out_specs=pl.BlockSpec(memory_space=pltpu.VMEM),
        scratch_shapes=[
            pltpu.SMEM((SLOTS,), jnp.int32),
            pltpu.SMEM((SLOTS,), jnp.int32),
            pltpu.SMEM((1,), jnp.int32),
            pltpu.SMEM((8, BS), jnp.int32),
            pltpu.VMEM((8, BS), jnp.int32),
            pltpu.VMEM((SLOTS, 2, NZ, 2, 8, BS), F32),
            pltpu.VMEM((SLOTS, 2 * BS, 2 * BS), BF16),
            pltpu.VMEM((2, SLOTS + 1, BS, BS), F32),
            pltpu.VMEM((NB, BS, BS), F32),
            pltpu.VMEM((NB, 2 * BS, 2 * BS), BF16),
            pltpu.VMEM((2, 16), F32),
            pltpu.VMEM((16, BS), F32),
            pltpu.VMEM((NZ, 16, BS), F32),
            pltpu.VMEM((2, BS, BS), BF16),
            pltpu.VMEM((NY, 2 * BS, BS), F32),
            pltpu.VMEM((NY, 2 * BS, BS), F32),
            pltpu.VMEM((2, 4, 2 * BS, BS), F32),
            pltpu.VMEM((2, 2, NZ, 8, BS), F32),
            pltpu.VMEM((2, NZ, 2, 8, BS), F32),
            pltpu.VMEM((2, NB, BS, BS), F32),
            pltpu.VMEM((NZ, 2, BS, BS), F32),
            pltpu.VMEM((256, 4096), BF16),
            pltpu.VMEM((256, 4096), BF16),
            pltpu.VMEM((NX, 8, 8, BS), F32),
            pltpu.VMEM((NX, 8, 8, BS), F32),
            pltpu.VMEM((NB, 8, 8, BS), F32),
            pltpu.SemaphoreType.DMA((7,)),
        ]
        + sems(12, 8, 8, 16, 16, 16, 32, 32, 32, 4, 12, 8),
        compiler_params=pltpu.CompilerParams(
            collective_id=0, has_side_effects=True, vmem_limit_bytes=56 * 2**20
        ),
        name="exchange",
    )(pair_mu, pair_nu, live_counts, tensor, orbitals, metric)


def solution(mesh):
    in_specs = (
        P("pair", "ri", None, None),
        P("pair"),
        P("pair"),
        P("pair"),
        P("pair", "batch"),
        P("ri", None),
    )
    return jax.shard_map(
        per_device,
        mesh=mesh,
        in_specs=in_specs,
        out_specs=P("pair", ("ri", "batch"), None),
        check_vma=False,
    )
```
